32 devices in a mesh: slab: 8 (over z, y), yz: 4 (over x, core).
Axes of the slice: x: 2, y: 2, z: 4, core: 2. Of those that a mesh axis runs over, the one named last changes fastest.
Arguments:
- grid_field: bfloat16 [32, 16, 256, 256], P(None, 'slab', 'yz'), may hold values from -6 to 6
- spectral_weight: bfloat16 [2, 32, 32, 8192], P(None, None, None, ('slab', 'yz')), may hold values from -24 to 24
- local_weight: bfloat16 [32, 32], replicated, may hold values from -1 to 1
Outputs:
- grad_field: bfloat16 [32, 16, 256, 256], P(None, 'slab', 'yz')
- grad_weight: float32 [2, 32, 32, 8192], P(None, None, None, ('slab', 'yz'))
The draws below stay inside these ranges and needn't reach their ends.
All inputs are finite; a program needn't handle non-finite values.
Results may differ from the reference program's by a relative error of at most 0.0075.
Values sent between devices are 32-bit elements; how exact they have to be, the bound alone decides.
No kernel may reach another device: no remote copies, remote signals or barrier semaphores. Data moves between devices by JAX's collectives and lax.ppermute only.
A program may use at most 64 MiB of HBM per device.

```python
import math
import jax
import jax.numpy as jnp
from jax import lax

C = 32
KX = 16
KY = 16
MZ = 32
NY = 256
NZ = 256
NX = 16
MODES = 8192
N_SLAB = 8
N_YZ = 4


def shard_levels(own_key, dims, pieces, least, high):
    loudness = 1.0
    for position, shards_of in pieces:
        heights = jax.random.uniform(jax.random.fold_in(jax.random.fold_in(own_key, 6), position), (shards_of,), jnp.float32, least / len(pieces), high / len(pieces))
        loudness = loudness * jnp.repeat(jnp.exp(heights), dims[position] // shards_of).reshape((-1,) + (1,) * (len(dims) - 1 - position))
    return loudness


def gaussian(rng, dims, scale, limit, cuts=(), held_as=jnp.bfloat16):
    drawn = scale * jax.random.normal(rng, dims, jnp.float32)
    if cuts:
        drawn = drawn * shard_levels(rng, dims, cuts, -0.22, 0.18)
    return jnp.clip(drawn, -limit, limit).astype(held_as)


def setup_inputs(seed: int = 0) -> dict:
    seeds = jax.random.split(jax.random.key(seed), 4)
    grid_field = gaussian(seeds[0], (C, NX, NY, NZ), 1.0, 6.0, ((1, 8), (2, 4)))
    spectral_weight = gaussian(seeds[1], (2, C, C, MODES), 4.0, 24.0, ((3, 32),))
    local_weight = gaussian(seeds[2], (C, C), C ** -0.5, 1.0)
    return {"grid_field": grid_field, "spectral_weight": spectral_weight, "local_weight": local_weight}


PRECISE = lax.Precision.HIGHEST
GELU_SCALE = 0.7978845608028654
GELU_CUBIC = 0.044715

def gelu_with_slope(before):
    inner_arg = GELU_SCALE * (before + GELU_CUBIC * before * before * before)
    tangent = jnp.tanh(inner_arg)
    values = 0.5 * before * (1.0 + tangent)
    slopes = 0.5 * (1.0 + tangent) + 0.5 * before * (1.0 - tangent * tangent) * GELU_SCALE * (1.0 + 3.0 * GELU_CUBIC * before * before)
    return (values, slopes)

def mode_freqs(number_modes, length):
    numbers = jnp.arange(number_modes, dtype=jnp.int32)
    return jnp.where(numbers < number_modes // 2, numbers, length - number_modes + numbers)

def twiddles(positions, frequencies, length):
    phases = positions[:, None] * frequencies[None, :] % length
    angles = phases.astype(jnp.float32) * (2.0 * math.pi / length)
    return (jnp.cos(angles), jnp.sin(angles))

def complex_einsum(pattern, left_real, left_imag, right_real, right_imag):

    def product(former, second):
        return jnp.einsum(pattern, former, second, precision=PRECISE)
    return (product(left_real, right_real) - product(left_imag, right_imag), product(left_real, right_imag) + product(left_imag, right_real))

def to_owner(cube):
    depth_groups = MZ // N_YZ
    pairs_dev = KY * depth_groups // N_SLAB
    shaped = cube.reshape(2, C, KX, KY, depth_groups, N_YZ)
    shaped = jnp.transpose(shaped, (0, 1, 3, 4, 5, 2))
    shaped = shaped.reshape(2, C, N_SLAB, pairs_dev, N_YZ, KX)
    shaped = jnp.transpose(shaped, (0, 1, 2, 4, 3, 5))
    return shaped.reshape(2, C, MODES)

def from_owner(listed):
    depth_groups = MZ // N_YZ
    pairs_dev = KY * depth_groups // N_SLAB
    shaped = listed.reshape(2, C, N_SLAB, N_YZ, pairs_dev, KX)
    shaped = jnp.transpose(shaped, (0, 1, 2, 4, 3, 5))
    shaped = shaped.reshape(2, C, KY, depth_groups, N_YZ, KX)
    shaped = jnp.transpose(shaped, (0, 1, 5, 2, 3, 4))
    return shaped.reshape(2, C, KX, KY, MZ)

def reference(grid_field, spectral_weight, local_weight):
    block_size = 8
    block_count = NX // block_size
    norm_scale = 1.0 / math.sqrt(NX * NY * NZ)
    y_frequencies = mode_freqs(KY, NY)
    x_frequencies = mode_freqs(KX, NX)
    depth_numbers = jnp.arange(MZ, dtype=jnp.int32)
    depth_double = jnp.where(depth_numbers == 0, 1.0, 2.0).astype(jnp.float32)
    local_float = local_weight.astype(jnp.float32)
    weight_real = spectral_weight[0].astype(jnp.float32)
    weight_imag = spectral_weight[1].astype(jnp.float32)
    block_ids = jnp.arange(block_count, dtype=jnp.int32)

    def analyze_block(block_field, start):
        depth_spec = jnp.fft.rfft(block_field, axis=3)[..., :MZ]
        pencil_spec = jnp.take(jnp.fft.fft(depth_spec, axis=2), y_frequencies, axis=2)
        positions = start + jnp.arange(block_size, dtype=jnp.int32)
        cosine_part, sine_part = twiddles(positions, x_frequencies, NX)
        plane_real, plane_imag = complex_einsum('cxjk,xm->cmjk', jnp.real(pencil_spec), jnp.imag(pencil_spec), cosine_part, -sine_part)
        return jnp.stack([plane_real, plane_imag])

    def synth_block(cube, start):
        positions = start + jnp.arange(block_size, dtype=jnp.int32)
        cosine_part, sine_part = twiddles(positions, x_frequencies, NX)
        plane_real, plane_imag = complex_einsum('cmjk,xm->cxjk', cube[0], cube[1], cosine_part, sine_part)
        spectrum = lax.complex(plane_real, plane_imag)
        padded = jnp.zeros((C, block_size, NY, NZ // 2 + 1), spectrum.dtype)
        padded = padded.at[:, :, y_frequencies, :MZ].set(spectrum)
        pencils = jnp.fft.ifft(padded, axis=2, norm='forward')
        return jnp.fft.irfft(pencils, n=NZ, axis=3, norm='forward')

    def take_block(start):
        return lax.dynamic_slice_in_dim(grid_field, start, block_size, 1)

    def first_pass(total, index):
        start = index * block_size
        piece = take_block(start).astype(jnp.float32)
        return (total + analyze_block(piece, start), index)
    zero_cube = jnp.zeros((2, C, KX, KY, MZ), jnp.float32)
    coef_cube = lax.scan(first_pass, zero_cube, block_ids)[0] * norm_scale
    coef_list = to_owner(coef_cube)
    mixed_real, mixed_imag = complex_einsum('oim,im->om', weight_real, weight_imag, coef_list[0], coef_list[1])
    mixed_cube = from_owner(jnp.stack([mixed_real, mixed_imag]))

    def second_pass(total, index):
        start = index * block_size
        piece = take_block(start).astype(jnp.float32)
        before = norm_scale * synth_block(mixed_cube, start) + jnp.einsum('oi,ixyz->oxyz', local_float, piece, precision=PRECISE)
        activation, slopes = gelu_with_slope(before)
        upstream = (activation * slopes).astype(jnp.bfloat16)
        return (total + analyze_block(upstream.astype(jnp.float32), start), upstream)
    back_sum, upstream_blocks = lax.scan(second_pass, zero_cube, block_ids)
    back_cube = back_sum * norm_scale * depth_double
    back_list = to_owner(back_cube)
    grad_real = jnp.einsum('om,im->oim', back_list[0], coef_list[0], precision=PRECISE) + jnp.einsum('om,im->oim', back_list[1], coef_list[1], precision=PRECISE)
    grad_imag = jnp.einsum('om,im->oim', back_list[1], coef_list[0], precision=PRECISE) - jnp.einsum('om,im->oim', back_list[0], coef_list[1], precision=PRECISE)
    grad_weight = jnp.stack([grad_real, grad_imag])
    modes_real = jnp.einsum('oim,om->im', weight_real, back_list[0], precision=PRECISE) + jnp.einsum('oim,om->im', weight_imag, back_list[1], precision=PRECISE)
    modes_imag = jnp.einsum('oim,om->im', weight_real, back_list[1], precision=PRECISE) - jnp.einsum('oim,om->im', weight_imag, back_list[0], precision=PRECISE)
    modes_cube = from_owner(jnp.stack([modes_real, modes_imag])) / depth_double

    def third_pass(carried, inputs):
        index, upstream = inputs
        start = index * block_size
        spectral_part = norm_scale * synth_block(modes_cube, start)
        local_part = jnp.einsum('oi,oxyz->ixyz', local_float, upstream.astype(jnp.float32), precision=PRECISE)
        return (carried, (spectral_part + local_part).astype(jnp.bfloat16))
    grad_blocks = lax.scan(third_pass, jnp.zeros((), jnp.float32), (block_ids, upstream_blocks))[1]
    grad_field = jnp.transpose(grad_blocks, (1, 0, 2, 3, 4)).reshape(C, NX, NY, NZ)
    return (grad_field, grad_weight)
```

```python
import math

import jax
import jax.numpy as jnp
import ml_dtypes
import numpy as np
from jax import lax
from jax.experimental import pallas as pl
from jax.experimental.pallas import tpu as pltpu
from jax.sharding import PartitionSpec as P

KX = 16
KY = 16
MZ = 32
NY = 256
NZ = 256
ROWS = 16

GELU_SCALE = 0.7978845608028654
GELU_CUBIC = 0.044715
BF16 = ml_dtypes.bfloat16


def freqs(number, length):
    index = np.arange(number)
    return np.where(index < number // 2, index, length - number + index)


def angles(positions, frequencies, length):
    phase = (positions[:, None].astype(np.int64) * frequencies[None, :]) % length
    return phase * (2.0 * math.pi / length)


def halves(matrix):
    matrix = np.asarray(matrix, np.float32)
    upper = matrix.astype(BF16)
    lower = (matrix - upper.astype(np.float32)).astype(BF16)
    return upper, lower


def depth_freqs(pencils):
    groups = MZ // pencils
    return np.array([[g * pencils + q for g in range(groups)] for q in range(pencils)])


def depth_analysis(pencils, doubled):
    kz = depth_freqs(pencils)
    theta = angles(kz.reshape(-1), np.arange(NZ), NZ).reshape(pencils, -1, NZ)
    weight = np.where(kz == 0, 1.0, 2.0 if doubled else 1.0)[:, :, None]
    table = np.stack([np.cos(theta) * weight, -np.sin(theta) * weight], axis=1)
    return np.concatenate(halves(table.reshape(2 * MZ, NZ)), axis=0)


def depth_synthesis(pencils, doubled):
    kz = depth_freqs(pencils)
    theta = angles(kz.reshape(-1), np.arange(NZ), NZ).reshape(pencils, -1, NZ)
    weight = np.where(kz == 0, 1.0, 2.0 if doubled else 1.0)[:, :, None]
    table = np.stack([np.cos(theta) * weight, -np.sin(theta) * weight], axis=1)
    upper, lower = halves(table.reshape(2 * MZ, NZ))
    return np.stack(
        [np.concatenate([upper, upper], 0), np.concatenate([lower, np.zeros_like(lower)], 0)]
    )


def row_analysis(pencils, planes):
    rows = NY // pencils
    tables = []
    for member in range(pencils):
        theta = angles(freqs(KY, NY), member * rows + np.arange(rows), NY)
        table = np.zeros((KY, 2, planes, 2, planes, rows))
        for x in range(planes):
            table[:, 0, x, 0, x] = np.cos(theta)
            table[:, 0, x, 1, x] = np.sin(theta)
            table[:, 1, x, 0, x] = -np.sin(theta)
            table[:, 1, x, 1, x] = np.cos(theta)
        table = table.reshape(KY * 2 * planes, 2 * planes * rows)
        tables.append(np.concatenate(halves(table), axis=0))
    return np.stack(tables)


def row_synthesis(pencils, planes):
    rows = NY // pencils
    tables = []
    for member in range(pencils):
        theta = angles(freqs(KY, NY), member * rows + np.arange(rows), NY)
        table = np.zeros((KY, 2, planes, 2, planes, rows))
        for x in range(planes):
            table[:, 0, x, 0, x] = np.cos(theta)
            table[:, 1, x, 0, x] = -np.sin(theta)
            table[:, 0, x, 1, x] = np.sin(theta)
            table[:, 1, x, 1, x] = np.cos(theta)
        upper, lower = halves(table.reshape(KY * 2 * planes, 2 * planes * rows))
        tables.append(np.concatenate([upper, upper, lower], axis=0))
    return np.stack(tables)


def plane_analysis(slabs, planes, kyn, scale):
    theta = angles(np.arange(slabs * planes), freqs(KX, slabs * planes), slabs * planes)
    theta = theta.reshape(slabs, planes, KX)
    table = np.zeros((slabs, kyn, 2, planes, 2, kyn, KX))
    for k in range(kyn):
        table[:, k, 0, :, 0, k] = np.cos(theta)
        table[:, k, 1, :, 0, k] = np.sin(theta)
        table[:, k, 0, :, 1, k] = -np.sin(theta)
        table[:, k, 1, :, 1, k] = np.cos(theta)
    upper, lower = halves(scale * table.reshape(slabs * kyn * 2 * planes, 2 * kyn * KX))
    return np.stack(
        [np.concatenate([upper, upper], 0), np.concatenate([lower, np.zeros_like(lower)], 0)]
    )


def plane_synthesis(slabs, planes, kyn, scale):
    theta = angles(np.arange(slabs * planes), freqs(KX, slabs * planes), slabs * planes)
    theta = theta.reshape(slabs, planes, KX)
    table = np.zeros((slabs, kyn, 2, planes, 2, kyn, KX))
    for k in range(kyn):
        table[:, k, 0, :, 0, k] = np.cos(theta)
        table[:, k, 0, :, 1, k] = -np.sin(theta)
        table[:, k, 1, :, 0, k] = np.sin(theta)
        table[:, k, 1, :, 1, k] = np.cos(theta)
    return np.stack(halves(scale * table.reshape(slabs * kyn * 2 * planes, 2 * kyn * KX)))


def channel_swap(channels, groups):
    table = np.zeros((groups, channels, channels, groups))
    for g in range(groups):
        for c in range(channels):
            table[g, c, c, g] = 1.0
    return table.reshape(groups * channels, channels * groups).astype(BF16)


def split(value):
    upper = value.astype(jnp.bfloat16)
    return upper, (value - upper.astype(jnp.float32)).astype(jnp.bfloat16)


def dot(left, right, left_dim=1, right_dim=0):
    return lax.dot_general(
        left, right, (((left_dim,), (right_dim,)), ((), ())), preferred_element_type=jnp.float32
    )


def analyze(grid_ref, depth_ref, row_ref, upper_ref, lower_ref, out_ref):
    channels, planes, rows, cells = grid_ref.shape
    slabs, pencils, chunk, _ = out_ref.shape
    groups = MZ // pencils
    width = planes * rows
    for c in range(0, channels, 2):
        block = grid_ref[c : c + 2].reshape(2 * width, cells)
        depth = dot(depth_ref[...], block, 1, 1)
        depth = depth[: 2 * MZ] + depth[2 * MZ :]
        for q in range(pencils):
            lines = []
            for e in range(2):
                base = q * 2 * groups
                lines.append(
                    jnp.concatenate(
                        [
                            depth[base : base + groups, e * width : (e + 1) * width],
                            depth[base + groups : base + 2 * groups, e * width : (e + 1) * width],
                        ],
                        axis=1,
                    )
                )
            upper, lower = split(jnp.concatenate(lines, axis=0))
            upper_ref[q, c * groups : (c + 2) * groups] = upper
            lower_ref[q, c * groups : (c + 2) * groups] = lower
    count = KY * 2 * planes
    for q in range(pencils):
        both = dot(row_ref[...], upper_ref[q], 1, 1)
        total = both[:count] + both[count:] + dot(row_ref[:count], lower_ref[q], 1, 1)
        out_ref[:, q] = total.reshape(slabs, chunk, channels * groups)


def analyze_kernel(grid_ref, depth_ref, row_ref, out_ref, upper_ref, lower_ref):
    analyze(grid_ref, depth_ref, row_ref, upper_ref, lower_ref, out_ref)


def collect(sums_ref, plane_ref, swap_ref, kyn):
    slabs, pencils, chunk, width = sums_ref.shape
    summed = sums_ref[:, 0]
    for member in range(1, pencils):
        summed = summed + sums_ref[:, member]
    summed = summed.reshape(slabs * chunk, width)
    stacked = jnp.concatenate(split(summed), axis=0)
    turned = dot(swap_ref[...], stacked, 1, 1).astype(jnp.bfloat16)
    coef = dot(turned, plane_ref[0]) + dot(turned, plane_ref[1])
    groups = chunk_groups(width, swap_ref)
    channels = width // groups
    parts = []
    for part in range(2):
        pieces = []
        for k in range(kyn):
            start = (part * kyn + k) * KX
            for g in range(groups):
                pieces.append(coef[g * channels : (g + 1) * channels, start : start + KX])
        parts.append(jnp.concatenate(pieces, axis=1) if len(pieces) > 1 else pieces[0])
    return parts


def chunk_groups(width, swap_ref):
    return width // CHANNELS


CHANNELS = 32


def distribute(real, imag, plane_ref, swap_ref, kyn, out_ref):
    slabs, pencils, chunk, width = out_ref.shape
    channels = real.shape[0]
    groups = width // channels
    lines = []
    for g in range(groups):
        pieces = []
        for value in (real, imag):
            for k in range(kyn):
                start = (k * groups + g) * KX
                pieces.append(value[:, start : start + KX])
        lines.append(jnp.concatenate(pieces, axis=1))
    upper, lower = split(jnp.concatenate(lines, axis=0))
    planes = (
        dot(plane_ref[0], upper, 1, 1)
        + dot(plane_ref[1], upper, 1, 1)
        + dot(plane_ref[0], lower, 1, 1)
    )
    stacked = jnp.concatenate(split(planes), axis=0)
    turned = dot(stacked, swap_ref[...])
    total = turned[: slabs * chunk] + turned[slabs * chunk :]
    total = total.reshape(slabs, chunk, width)
    for member in range(pencils):
        out_ref[:, member] = total


def mix_kernel(kyn, sums_ref, weight_ref, ahead_ref, back_ref, swap_ref, out_ref, coef_ref, mixed_ref):
    real, imag = collect(sums_ref, ahead_ref, swap_ref, kyn)
    coef_ref[0] = real
    coef_ref[1] = imag
    for o in range(weight_ref.shape[1]):
        weight_real = weight_ref[0, o].astype(jnp.float32)
        weight_imag = weight_ref[1, o].astype(jnp.float32)
        mixed_ref[0, o : o + 1] = jnp.sum(
            weight_real * real - weight_imag * imag, axis=0, keepdims=True
        )
        mixed_ref[1, o : o + 1] = jnp.sum(
            weight_real * imag + weight_imag * real, axis=0, keepdims=True
        )
    distribute(mixed_ref[0], mixed_ref[1], back_ref, swap_ref, kyn, out_ref)


def unmix_kernel(kyn, sums_ref, weight_ref, ahead_ref, back_ref, swap_ref, out_ref, coef_ref):
    real, imag = collect(sums_ref, ahead_ref, swap_ref, kyn)
    coef_ref[0] = real
    coef_ref[1] = imag
    modes_real = jnp.zeros_like(real)
    modes_imag = jnp.zeros_like(real)
    for o in range(weight_ref.shape[1]):
        weight_real = weight_ref[0, o].astype(jnp.float32)
        weight_imag = weight_ref[1, o].astype(jnp.float32)
        back_real = coef_ref[0, o : o + 1]
        back_imag = coef_ref[1, o : o + 1]
        modes_real = modes_real + (weight_real * back_real + weight_imag * back_imag)
        modes_imag = modes_imag + (weight_real * back_imag - weight_imag * back_real)
    distribute(modes_real, modes_imag, back_ref, swap_ref, kyn, out_ref)


def outer_kernel(coef_ref, back_ref, out_ref):
    real, imag = coef_ref[0], coef_ref[1]
    for o in range(back_ref.shape[1]):
        back_real = back_ref[0, o : o + 1]
        back_imag = back_ref[1, o : o + 1]
        out_ref[0, o] = back_real * real + back_imag * imag
        out_ref[1, o] = back_imag * real - back_real * imag


def lift(values_ref, row_ref, spread_ref):
    slabs, pencils, chunk, width = values_ref.shape
    groups = MZ // pencils
    channels = width // groups
    lines = []
    for q in range(pencils):
        value = values_ref[:, q].reshape(slabs * chunk, width)
        upper, lower = split(value)
        stacked = jnp.concatenate([upper, lower, upper], axis=0)
        lines.append(dot(stacked, row_ref[...], 0, 0))
    lanes = lines[0].shape[1] // 2
    for o in range(channels):
        pieces = []
        for q in range(pencils):
            for part in range(2):
                pieces.append(
                    lines[q][o * groups : (o + 1) * groups, part * lanes : (part + 1) * lanes]
                )
        block = jnp.concatenate(pieces, axis=0)
        upper = block.astype(jnp.bfloat16).astype(jnp.float32)
        both = jnp.concatenate([upper, block - upper], axis=0)
        spread_ref[o * lanes : (o + 1) * lanes] = both.T.astype(jnp.bfloat16)


def tile_sums(spread_ref, grid_ref, depth_ref, local_ref, x, y):
    channels, planes, rows, cells = grid_ref.shape
    block = grid_ref[:, x, pl.ds(y, ROWS)].reshape(channels * ROWS, cells)
    spread = spread_ref[:, x, pl.ds(y, ROWS)].reshape(channels * ROWS, 4 * MZ)
    return dot(local_ref[...], block) + dot(spread, depth_ref[0]) + dot(spread, depth_ref[1])


def middle_kernel(
    values_ref, grid_ref, local_ref, lift_ref, synth_ref, depth_ref, row_ref,
    up_ref, out_ref, spread_ref, upper_ref, lower_ref,
):
    channels, planes, rows, cells = grid_ref.shape
    lift(values_ref, lift_ref, spread_ref)
    spread = spread_ref.reshape(channels, planes, rows, 4 * MZ)

    def step(index, carry):
        x = index // (rows // ROWS)
        y = pl.multiple_of((index % (rows // ROWS)) * ROWS, ROWS)
        before = tile_sums(spread, grid_ref, synth_ref, local_ref, x, y)
        square = before * before
        inner = before * (GELU_SCALE + (GELU_SCALE * GELU_CUBIC) * square)
        gate = 0.5 + 0.5 * jnp.tanh(inner)
        twice = 2.0 * GELU_SCALE + (6.0 * GELU_SCALE * GELU_CUBIC) * square
        slope = 1.0 + before * (1.0 - gate) * twice
        upstream = (before * gate) * (gate * slope)
        up_ref[:, x, pl.ds(y, ROWS)] = upstream.astype(jnp.bfloat16).reshape(channels, ROWS, cells)
        return carry

    lax.fori_loop(0, planes * (rows // ROWS), step, 0)
    analyze(up_ref, depth_ref, row_ref, upper_ref, lower_ref, out_ref)


def final_kernel(values_ref, grid_ref, local_ref, lift_ref, synth_ref, out_ref, spread_ref):
    channels, planes, rows, cells = grid_ref.shape
    lift(values_ref, lift_ref, spread_ref)
    spread = spread_ref.reshape(channels, planes, rows, 4 * MZ)

    def step(index, carry):
        x = index // (rows // ROWS)
        y = pl.multiple_of((index % (rows // ROWS)) * ROWS, ROWS)
        total = tile_sums(spread, grid_ref, synth_ref, local_ref, x, y)
        out_ref[:, x, pl.ds(y, ROWS)] = total.astype(jnp.bfloat16).reshape(channels, ROWS, cells)
        return carry

    lax.fori_loop(0, planes * (rows // ROWS), step, 0)


VMEM = pl.BlockSpec(memory_space=pltpu.VMEM)


def call(kernel, outs, scratch, *operands, flops=1 << 30, size=4 << 20):
    return pl.pallas_call(
        kernel,
        out_shape=outs,
        in_specs=[VMEM] * len(operands),
        out_specs=jax.tree.map(lambda _: VMEM, outs),
        scratch_shapes=scratch,
        compiler_params=pltpu.CompilerParams(vmem_limit_bytes=40 << 20),
        cost_estimate=pl.CostEstimate(flops=flops, bytes_accessed=size, transcendentals=0),
    )(*operands)


def f32(*shape):
    return jax.ShapeDtypeStruct(shape, jnp.float32)


def bf16(*shape):
    return jax.ShapeDtypeStruct(shape, jnp.bfloat16)


def on_device(grid_field, spectral_weight, local_weight):
    channels, planes, rows, cells = grid_field.shape
    slabs = lax.axis_size("slab")
    pencils = lax.axis_size("yz")
    groups = MZ // pencils
    member = lax.axis_index("yz")
    scale = 1.0 / math.sqrt(planes * slabs * NY * NZ)
    pairs = KY * groups // slabs
    kyn = max(1, pairs // groups)
    gn = pairs // kyn
    blocks = KY // kyn
    turns = groups // gn
    lanes = channels * groups
    line = kyn * 2 * planes
    modes = spectral_weight.shape[3]

    row_ahead = lax.dynamic_index_in_dim(jnp.asarray(row_analysis(pencils, planes)), member, 0, False)
    row_back = lax.dynamic_index_in_dim(jnp.asarray(row_synthesis(pencils, planes)), member, 0, False)
    plane_ahead = jnp.asarray(plane_analysis(slabs, planes, kyn, scale))
    plane_back = jnp.asarray(plane_synthesis(slabs, planes, kyn, scale))
    swap = jnp.asarray(channel_swap(channels, gn))
    repeat = jnp.asarray(np.repeat(np.eye(channels), ROWS, axis=0).astype(BF16))
    mask = jnp.asarray(np.tile(np.eye(ROWS), (channels, channels)).astype(BF16))

    def widen(weight):
        rows_wide = dot(repeat, weight).astype(jnp.bfloat16)
        return dot(rows_wide, repeat, 1, 1).astype(jnp.bfloat16) * mask

    def to_owner(parts):
        if turns > 1:
            parts = parts.reshape(blocks, pencils, line, channels, turns, gn)
            parts = jnp.transpose(parts, (0, 4, 1, 2, 3, 5))
        parts = parts.reshape(slabs * pencils, line, channels * gn)
        moved = lax.all_to_all(parts, ("slab", "yz"), 0, 0, tiled=True)
        return moved.reshape(slabs, pencils, line, channels * gn)

    def from_owner(values):
        values = values.reshape(slabs * pencils, line, channels * gn)
        moved = lax.all_to_all(values, ("slab", "yz"), 0, 0, tiled=True)
        if turns > 1:
            moved = moved.reshape(blocks, turns, pencils, line, channels, gn)
            moved = jnp.transpose(moved, (0, 2, 3, 4, 1, 5))
        return moved.reshape(blocks, pencils, line, lanes)

    halves_scratch = [pltpu.VMEM((pencils, lanes, 2 * planes * rows), jnp.bfloat16)] * 2
    spread_scratch = pltpu.VMEM((channels * planes * rows, 4 * MZ), jnp.bfloat16)
    sent = f32(blocks, pencils, line, lanes)
    given = f32(slabs, pencils, line, channels * gn)
    coefs = f32(2, channels, modes)

    parts = call(
        analyze_kernel, sent, halves_scratch,
        grid_field, jnp.asarray(depth_analysis(pencils, False)), row_ahead,
    )
    received = to_owner(parts)

    def mix(*refs):
        mix_kernel(kyn, *refs)

    values, coef = call(
        mix, (given, coefs), [pltpu.VMEM((2, channels, modes), jnp.float32)],
        received, spectral_weight, plane_ahead, plane_back, swap,
    )
    upstream, parts = call(
        middle_kernel,
        (bf16(channels, planes, rows, cells), sent),
        [spread_scratch] + halves_scratch,
        from_owner(values), grid_field, widen(local_weight), row_back,
        jnp.asarray(depth_synthesis(pencils, True)), jnp.asarray(depth_analysis(pencils, True)), row_ahead,
    )
    received = to_owner(parts)

    def unmix(*refs):
        unmix_kernel(kyn, *refs)

    values, back = call(
        unmix, (given, coefs), [],
        received, spectral_weight, plane_ahead, plane_back, swap,
    )
    grad_weight = call(outer_kernel, f32(2, channels, channels, modes), [], coef, back)
    grad_field = call(
        final_kernel, bf16(channels, planes, rows, cells), [spread_scratch],
        from_owner(values), upstream, widen(local_weight.T), row_back,
        jnp.asarray(depth_synthesis(pencils, False)),
    )
    return grad_field, grad_weight


def solution(mesh):
    return jax.shard_map(
        on_device,
        mesh=mesh,
        in_specs=(P(None, "slab", "yz", None), P(None, None, None, ("slab", "yz")), P()),
        out_specs=(P(None, "slab", "yz", None), P(None, None, None, ("slab", "yz"))),
        check_vma=False,
    )
```

```python
import math

import jax
import jax.numpy as jnp
import ml_dtypes
import numpy as np
from jax import lax
from jax.experimental import pallas as pl
from jax.experimental.pallas import tpu as pltpu
from jax.sharding import PartitionSpec as P

KX = 16
KY = 16
MZ = 32
NY = 256
NZ = 256
ROWS = 16
PIECES = 2

GELU_SCALE = 0.7978845608028654
GELU_CUBIC = 0.044715
BF16 = ml_dtypes.bfloat16
LARGE = 53248


def freqs(number, length):
    index = np.arange(number)
    return np.where(index < number // 2, index, length - number + index)


def angles(positions, frequencies, length):
    phase = (positions[:, None].astype(np.int64) * frequencies[None, :]) % length
    return phase * (2.0 * math.pi / length)


def halves(matrix):
    matrix = np.asarray(matrix, np.float32)
    upper = matrix.astype(BF16)
    lower = (matrix - upper.astype(np.float32)).astype(BF16)
    return upper, lower


def depth_freqs(pencils):
    groups = MZ // pencils
    return np.array([[g * pencils + q for g in range(groups)] for q in range(pencils)])


def depth_analysis(pencils, doubled):
    kz = depth_freqs(pencils)
    theta = angles(kz.reshape(-1), np.arange(NZ), NZ).reshape(pencils, -1, NZ)
    weight = np.where(kz == 0, 1.0, 2.0 if doubled else 1.0)[:, :, None]
    table = np.stack([np.cos(theta) * weight, -np.sin(theta) * weight], axis=1)
    return np.concatenate(halves(table.reshape(2 * MZ, NZ)), axis=0)


def depth_synthesis(pencils, doubled):
    kz = depth_freqs(pencils)
    theta = angles(kz.reshape(-1), np.arange(NZ), NZ).reshape(pencils, -1, NZ)
    weight = np.where(kz == 0, 1.0, 2.0 if doubled else 1.0)[:, :, None]
    table = np.stack([np.cos(theta) * weight, -np.sin(theta) * weight], axis=1)
    return np.tile(table.reshape(2 * MZ, NZ), (2, 1)).astype(BF16)


def row_analysis(pencils, planes):
    rows = NY // pencils
    tables = []
    for member in range(pencils):
        theta = angles(freqs(KY, NY), member * rows + np.arange(rows), NY)
        table = np.zeros((KY, 2, planes, 2, planes, rows))
        for x in range(planes):
            table[:, 0, x, 0, x] = np.cos(theta)
            table[:, 0, x, 1, x] = np.sin(theta)
            table[:, 1, x, 0, x] = -np.sin(theta)
            table[:, 1, x, 1, x] = np.cos(theta)
        table = table.reshape(KY * 2 * planes, 2 * planes * rows)
        tables.append(np.concatenate(halves(table), axis=0))
    return np.stack(tables)


def row_synthesis(pencils, planes):
    rows = NY // pencils
    tables = []
    for member in range(pencils):
        theta = angles(freqs(KY, NY), member * rows + np.arange(rows), NY)
        table = np.zeros((KY, 2, planes, 2, planes, rows))
        for x in range(planes):
            table[:, 0, x, 0, x] = np.cos(theta)
            table[:, 1, x, 0, x] = -np.sin(theta)
            table[:, 0, x, 1, x] = np.sin(theta)
            table[:, 1, x, 1, x] = np.cos(theta)
        upper, lower = halves(table.reshape(KY * 2 * planes, 2 * planes * rows))
        tables.append(np.concatenate([upper, upper, lower], axis=0))
    return np.stack(tables)


def plane_analysis(slabs, planes, kyn, scale):
    theta = angles(np.arange(slabs * planes), freqs(KX, slabs * planes), slabs * planes)
    theta = theta.reshape(slabs, planes, KX)
    table = np.zeros((slabs, kyn, 2, planes, 2, kyn, KX))
    for k in range(kyn):
        table[:, k, 0, :, 0, k] = np.cos(theta)
        table[:, k, 1, :, 0, k] = np.sin(theta)
        table[:, k, 0, :, 1, k] = -np.sin(theta)
        table[:, k, 1, :, 1, k] = np.cos(theta)
    upper, lower = halves(scale * table.reshape(slabs * kyn * 2 * planes, 2 * kyn * KX))
    return np.stack(
        [np.concatenate([upper, upper], 0), np.concatenate([lower, np.zeros_like(lower)], 0)]
    )


def plane_synthesis(slabs, planes, kyn, scale):
    theta = angles(np.arange(slabs * planes), freqs(KX, slabs * planes), slabs * planes)
    theta = theta.reshape(slabs, planes, KX)
    table = np.zeros((slabs, kyn, 2, planes, 2, kyn, KX))
    for k in range(kyn):
        table[:, k, 0, :, 0, k] = np.cos(theta)
        table[:, k, 0, :, 1, k] = -np.sin(theta)
        table[:, k, 1, :, 0, k] = np.sin(theta)
        table[:, k, 1, :, 1, k] = np.cos(theta)
    return np.stack(halves(scale * table.reshape(slabs * kyn * 2 * planes, 2 * kyn * KX)))


def channel_swap(channels, groups):
    table = np.zeros((groups, channels, channels, groups))
    for g in range(groups):
        for c in range(channels):
            table[g, c, c, g] = 1.0
    return table.reshape(groups * channels, channels * groups).astype(BF16)


def split(value):
    upper = value.astype(jnp.bfloat16)
    return upper, (value - upper.astype(jnp.float32)).astype(jnp.bfloat16)


def dot(left, right, left_dim=1, right_dim=0):
    return lax.dot_general(
        left, right, (((left_dim,), (right_dim,)), ((), ())), preferred_element_type=jnp.float32
    )


def analyze(grid_ref, depth_ref, row_ref, upper_ref, lower_ref, kept_ref, sent_ref, ready):
    channels, planes, rows, cells = grid_ref.shape
    blocks, pencils, line, half = kept_ref.shape
    groups = MZ // pencils
    width = planes * rows
    for c in range(0, channels, 2):
        ready(c)
        block = grid_ref[c : c + 2].reshape(2 * width, cells)
        depth = dot(depth_ref[...], block, 1, 1)
        depth = depth[: 2 * MZ] + depth[2 * MZ :]
        for q in range(pencils):
            lines = []
            for e in range(2):
                base = q * 2 * groups
                lines.append(
                    jnp.concatenate(
                        [
                            depth[base : base + groups, e * width : (e + 1) * width],
                            depth[base + groups : base + 2 * groups, e * width : (e + 1) * width],
                        ],
                        axis=1,
                    )
                )
            upper, lower = split(jnp.concatenate(lines, axis=0))
            upper_ref[q, c * groups : (c + 2) * groups] = upper
            lower_ref[q, c * groups : (c + 2) * groups] = lower
    ready(channels)
    count = KY * 2 * planes
    first = lax.axis_index("yz") % 2 == 0
    for q in range(pencils):
        both = dot(row_ref[...], upper_ref[q], 1, 1)
        total = both[:count] + both[count:] + dot(row_ref[:count], lower_ref[q], 1, 1)
        low = total[:, :half].reshape(blocks, line, half)
        high = total[:, half:].reshape(blocks, line, half)
        kept_ref[:, q] = jnp.where(first, low, high)
        sent_ref[:, q] = jnp.where(first, high, low)


def analyze_kernel(
    grid_hbm, depth_hbm, row_hbm, kept_ref, sent_ref,
    grid_ref, depth_ref, row_ref, upper_ref, lower_ref, piece_sem, table_sem,
):
    channels = grid_hbm.shape[0]
    step = channels // PIECES
    member = lax.axis_index("yz")
    depth_copy = pltpu.make_async_copy(depth_hbm, depth_ref, table_sem.at[0])
    row_copy = pltpu.make_async_copy(row_hbm.at[member], row_ref, table_sem.at[1])
    pieces = [
        pltpu.make_async_copy(
            grid_hbm.at[pl.ds(i * step, step)], grid_ref.at[pl.ds(i * step, step)], piece_sem.at[i]
        )
        for i in range(PIECES)
    ]
    depth_copy.start()
    for piece in pieces:
        piece.start()
    row_copy.start()
    depth_copy.wait()

    def ready(c):
        if c == channels:
            row_copy.wait()
        elif c % step == 0:
            pieces[c // step].wait()

    analyze(grid_ref, depth_ref, row_ref, upper_ref, lower_ref, kept_ref, sent_ref, ready)


def collect(sums_ref, plane_ref, swap_ref, kyn, channels):
    slabs, pencils, line, half = sums_ref.shape
    sides = []
    for core in range(2):
        side = sums_ref[:, core]
        for member in range(core + 2, pencils, 2):
            side = side + sums_ref[:, member]
        sides.append(side.reshape(slabs * line, half))
    stacked = jnp.concatenate(split(jnp.concatenate(sides, axis=1)), axis=0)
    turned = dot(swap_ref[...], stacked, 1, 1).astype(jnp.bfloat16)
    coef = dot(turned, plane_ref[0]) + dot(turned, plane_ref[1])
    groups = 2 * half // channels
    parts = []
    for part in range(2):
        pieces = []
        for k in range(kyn):
            start = (part * kyn + k) * KX
            for g in range(groups):
                pieces.append(coef[g * channels : (g + 1) * channels, start : start + KX])
        parts.append(jnp.concatenate(pieces, axis=1) if len(pieces) > 1 else pieces[0])
    return parts


def distribute(real, imag, plane_ref, swap_ref, kyn, out_ref):
    slabs, pencils, line, half = out_ref.shape
    channels = real.shape[0]
    groups = 2 * half // channels
    lines = []
    for g in range(groups):
        pieces = []
        for value in (real, imag):
            for k in range(kyn):
                start = (k * groups + g) * KX
                pieces.append(value[:, start : start + KX])
        lines.append(jnp.concatenate(pieces, axis=1))
    upper, lower = split(jnp.concatenate(lines, axis=0))
    planes = (
        dot(plane_ref[0], upper, 1, 1)
        + dot(plane_ref[1], upper, 1, 1)
        + dot(plane_ref[0], lower, 1, 1)
    )
    stacked = jnp.concatenate(split(planes), axis=0)
    turned = dot(stacked, swap_ref[...])
    total = turned[: slabs * line] + turned[slabs * line :]
    for member in range(pencils):
        side = total[:, member % 2 * half : (member % 2 + 1) * half]
        out_ref[:, member] = side.reshape(slabs, line, half)


def mix_kernel(
    kyn, sums_ref, weight_ref, ahead_ref, back_ref, swap_ref, out_ref, coef_hbm, coef_ref, mixed_ref, sem
):
    real, imag = collect(sums_ref, ahead_ref, swap_ref, kyn, weight_ref.shape[1])
    coef_ref[0] = real
    coef_ref[1] = imag
    copy = pltpu.make_async_copy(coef_ref, coef_hbm, sem)
    copy.start()
    for o in range(weight_ref.shape[1]):
        weight_real = weight_ref[0, o].astype(jnp.float32)
        weight_imag = weight_ref[1, o].astype(jnp.float32)
        mixed_ref[0, o : o + 1] = jnp.sum(
            weight_real * real - weight_imag * imag, axis=0, keepdims=True
        )
        mixed_ref[1, o : o + 1] = jnp.sum(
            weight_real * imag + weight_imag * real, axis=0, keepdims=True
        )
    distribute(mixed_ref[0], mixed_ref[1], back_ref, swap_ref, kyn, out_ref)
    copy.wait()


def unmix_kernel(kyn, sums_ref, weight_ref, ahead_ref, back_ref, swap_ref, out_ref, coef_ref):
    real, imag = collect(sums_ref, ahead_ref, swap_ref, kyn, weight_ref.shape[1])
    coef_ref[0] = real
    coef_ref[1] = imag
    modes_real = jnp.zeros_like(real)
    modes_imag = jnp.zeros_like(real)
    for o in range(weight_ref.shape[1]):
        weight_real = weight_ref[0, o].astype(jnp.float32)
        weight_imag = weight_ref[1, o].astype(jnp.float32)
        back_real = coef_ref[0, o : o + 1]
        back_imag = coef_ref[1, o : o + 1]
        modes_real = modes_real + (weight_real * back_real + weight_imag * back_imag)
        modes_imag = modes_imag + (weight_real * back_imag - weight_imag * back_real)
    distribute(modes_real, modes_imag, back_ref, swap_ref, kyn, out_ref)


def outer_kernel(coef_ref, back_ref, out_ref):
    real, imag = coef_ref[0], coef_ref[1]
    for o in range(back_ref.shape[1]):
        back_real = back_ref[0, o : o + 1]
        back_imag = back_ref[1, o : o + 1]
        out_ref[0, o] = back_real * real + back_imag * imag
        out_ref[1, o] = back_imag * real - back_real * imag


def lift(mine_ref, other_ref, row_ref, spread_ref):
    blocks, pencils, line, half = mine_ref.shape
    groups = MZ // pencils
    channels = 2 * half // groups
    first = lax.axis_index("yz") % 2 == 0
    lines = []
    for q in range(pencils):
        mine = mine_ref[:, q].reshape(blocks * line, half)
        other = other_ref[:, q].reshape(blocks * line, half)
        value = jnp.concatenate(
            [jnp.where(first, mine, other), jnp.where(first, other, mine)], axis=1
        )
        upper, lower = split(value)
        stacked = jnp.concatenate([upper, lower, upper], axis=0)
        lines.append(dot(stacked, row_ref[...], 0, 0))
    lanes = lines[0].shape[1] // 2
    for o in range(channels):
        pieces = []
        for q in range(pencils):
            for part in range(2):
                pieces.append(
                    lines[q][o * groups : (o + 1) * groups, part * lanes : (part + 1) * lanes]
                )
        block = jnp.concatenate(pieces, axis=0)
        upper = block.astype(jnp.bfloat16).astype(jnp.float32)
        both = jnp.concatenate([upper, block - upper], axis=0)
        spread_ref[o * lanes : (o + 1) * lanes] = both.T.astype(jnp.bfloat16)


def tile(ref, x, y):
    return ref[:, x, y : y + ROWS].reshape(ref.shape[0] * ROWS, ref.shape[3])


def fetch(hbm, ref, sem):
    copy = pltpu.make_async_copy(hbm, ref, sem)
    copy.start()
    return copy


def tiles(ref):
    for x in range(ref.shape[1]):
        for y in range(0, ref.shape[2], ROWS):
            yield x, y


def local_kernel(grid_ref, wide_ref, out_ref):
    channels, planes, rows, cells = grid_ref.shape
    for x, y in tiles(grid_ref):
        total = dot(wide_ref[...], tile(grid_ref, x, y))
        out_ref[:, x, y : y + ROWS] = total.reshape(channels, ROWS, cells)


def middle_kernel(
    mine_ref, other_ref, local_ref, lift_ref, synth_ref, depth_ref, row_hbm,
    up_ref, kept_ref, sent_ref, spread_ref, row_ref, upper_ref, lower_ref, row_sem,
):
    channels, planes, rows, cells = local_ref.shape
    row_copy = fetch(row_hbm.at[lax.axis_index("yz")], row_ref, row_sem)
    lift(mine_ref, other_ref, lift_ref, spread_ref)
    spread = spread_ref.reshape(channels, planes, rows, 4 * MZ)
    for x, y in tiles(local_ref):
        before = dot(tile(spread, x, y), synth_ref[...]) + tile(local_ref, x, y)
        square = before * before
        inner = before * (GELU_SCALE + (GELU_SCALE * GELU_CUBIC) * square)
        gate = 0.5 + 0.5 * jnp.tanh(inner)
        twice = 2.0 * GELU_SCALE + (6.0 * GELU_SCALE * GELU_CUBIC) * square
        slope = 1.0 + before * (1.0 - gate) * twice
        upstream = (before * gate) * (gate * slope)
        upstream = upstream.astype(jnp.bfloat16).reshape(channels, ROWS, cells)
        up_ref[:, x, y : y + ROWS] = upstream

    def ready(c):
        if c == channels:
            row_copy.wait()

    analyze(up_ref, depth_ref, row_ref, upper_ref, lower_ref, kept_ref, sent_ref, ready)


def final_kernel(
    mine_ref, other_ref, local_ref, lift_ref, synth_ref, out_hbm, spread_ref, result_ref, out_sems
):
    channels, planes, rows, cells = local_ref.shape
    lift(mine_ref, other_ref, lift_ref, spread_ref)
    spread = spread_ref.reshape(channels, planes, rows, 4 * MZ)
    copies = []
    for x, y in tiles(local_ref):
        total = dot(tile(spread, x, y), synth_ref[...]) + tile(local_ref, x, y)
        total = total.astype(jnp.bfloat16).reshape(channels, ROWS, cells)
        result_ref[:, x, y : y + ROWS] = total
        copies.append(
            fetch(
                result_ref.at[:, x, pl.ds(y, ROWS)],
                out_hbm.at[:, x, pl.ds(y, ROWS)],
                out_sems.at[len(copies)],
            )
        )
    for copy in copies:
        copy.wait()


VMEM = pl.BlockSpec(memory_space=pltpu.VMEM)
HBM = pl.BlockSpec(memory_space=pltpu.HBM)


def call(kernel, outs, scratch, *operands, far=(), out_specs=None, limit=20480):
    return pl.pallas_call(
        kernel,
        out_shape=outs,
        in_specs=[HBM if i in far else VMEM for i in range(len(operands))],
        out_specs=jax.tree.map(lambda _: VMEM, outs) if out_specs is None else out_specs,
        scratch_shapes=scratch,
        compiler_params=pltpu.CompilerParams(vmem_limit_bytes=limit << 10),
        cost_estimate=pl.CostEstimate(flops=1 << 30, bytes_accessed=4 << 20, transcendentals=0),
    )(*operands)


def f32(*shape):
    return jax.ShapeDtypeStruct(shape, jnp.float32)


def bf16(*shape):
    return jax.ShapeDtypeStruct(shape, jnp.bfloat16)


def on_device(grid_field, spectral_weight, local_weight):
    channels, planes, rows, cells = grid_field.shape
    slabs = lax.axis_size("slab")
    pencils = lax.axis_size("yz")
    groups = MZ // pencils
    member = lax.axis_index("yz")
    scale = 1.0 / math.sqrt(planes * slabs * NY * NZ)
    pairs = KY * groups // slabs
    kyn = max(1, pairs // groups)
    gn = pairs // kyn
    blocks = KY // kyn
    turns = groups // gn
    half = channels // 2
    line = kyn * 2 * planes
    modes = spectral_weight.shape[3]

    row_ahead = jnp.asarray(row_analysis(pencils, planes))
    row_back = lax.dynamic_index_in_dim(jnp.asarray(row_synthesis(pencils, planes)), member, 0, False)
    plane_ahead = jnp.asarray(plane_analysis(slabs, planes, kyn, scale))
    plane_back = jnp.asarray(plane_synthesis(slabs, planes, kyn, scale))
    swap = jnp.asarray(channel_swap(channels, gn))
    repeat = jnp.asarray(np.repeat(np.eye(channels), ROWS, axis=0).astype(BF16))
    mask = jnp.asarray(np.tile(np.eye(ROWS), (channels, channels)).astype(BF16))
    neighbours = [(i, i ^ 1) for i in range(pencils)]

    def widen(weight):
        rows_wide = dot(repeat, weight).astype(jnp.bfloat16)
        return dot(rows_wide, repeat, 1, 1).astype(jnp.bfloat16) * mask

    def to_owner(kept, sent, beside):
        given = lax.ppermute(sent, "yz", neighbours)
        given, beside = lax.optimization_barrier((given, beside))
        parts = kept + given
        if turns > 1:
            parts = parts.reshape(blocks, pencils, line, half, turns, gn)
            parts = jnp.transpose(parts, (0, 4, 1, 2, 3, 5))
        parts = parts.reshape(slabs * pencils, line, half * gn)
        moved = lax.all_to_all(parts, ("slab", "yz"), 0, 0, tiled=True)
        return moved.reshape(slabs, pencils, line, half * gn), beside

    def from_owner(values, work):
        values = values.reshape(slabs * pencils, line, half * gn)
        moved = lax.all_to_all(values, ("slab", "yz"), 0, 0, tiled=True)
        if turns > 1:
            moved = moved.reshape(blocks, turns, pencils, line, half, gn)
            moved = jnp.transpose(moved, (0, 2, 3, 4, 1, 5))
        moved = moved.reshape(blocks, pencils, line, half * groups)
        other = lax.ppermute(moved, "yz", neighbours)
        if work is None:
            return moved, other, None
        return lax.optimization_barrier((moved, other, work(moved)))

    halves_scratch = [pltpu.VMEM((pencils, channels * groups, 2 * planes * rows), jnp.bfloat16)] * 2
    row_scratch = pltpu.VMEM(row_ahead.shape[1:], jnp.bfloat16)
    spread_scratch = pltpu.VMEM((channels * planes * rows, 4 * MZ), jnp.bfloat16)
    field_scratch = pltpu.VMEM(grid_field.shape, jnp.bfloat16)
    sums = f32(blocks, pencils, line, half * groups)
    given = f32(slabs, pencils, line, half * gn)
    coefs = f32(2, channels, modes)
    depth_ahead = jnp.asarray(depth_analysis(pencils, False))

    kept, sent = call(
        analyze_kernel, (sums, sums),
        [
            field_scratch, pltpu.VMEM(depth_ahead.shape, jnp.bfloat16), row_scratch, *halves_scratch,
            pltpu.SemaphoreType.DMA((PIECES,)), pltpu.SemaphoreType.DMA((2,)),
        ],
        grid_field, depth_ahead, row_ahead, far=(0, 1, 2), limit=LARGE + 1536,
    )
    received, (wide, wide_back, row_back) = to_owner(
        kept, sent, (widen(local_weight), widen(local_weight.T), row_back)
    )

    def mix(*refs):
        mix_kernel(kyn, *refs)

    values, coef = call(
        mix, (given, coefs),
        [pltpu.VMEM((2, channels, modes), jnp.float32)] * 2 + [pltpu.SemaphoreType.DMA],
        received, spectral_weight, plane_ahead, plane_back, swap, out_specs=(VMEM, HBM),
    )
    def local_ahead(moved):
        _, late = lax.optimization_barrier((moved, wide))
        return call(local_kernel, f32(*grid_field.shape), [], grid_field, late)

    mine, other, local = from_owner(values, local_ahead)
    upstream, kept, sent = call(
        middle_kernel, (bf16(*grid_field.shape), sums, sums),
        [spread_scratch, row_scratch, *halves_scratch, pltpu.SemaphoreType.DMA],
        mine, other, local, row_back,
        jnp.asarray(depth_synthesis(pencils, True)), jnp.asarray(depth_analysis(pencils, True)), row_ahead,
        far=(6,),
    )
    received, local = to_owner(
        kept, sent, call(local_kernel, f32(*grid_field.shape), [], upstream, wide_back)
    )

    def unmix(*refs):
        unmix_kernel(kyn, *refs)

    values, back = call(
        unmix, (given, coefs), [],
        received, spectral_weight, plane_ahead, plane_back, swap,
    )

    def outer(moved):
        _, late = lax.optimization_barrier((moved, back))
        return call(outer_kernel, f32(2, channels, channels, modes), [], coef, late)

    mine, other, grad_weight = from_owner(values, outer)
    grad_field = call(
        final_kernel, bf16(*grid_field.shape),
        [spread_scratch, field_scratch, pltpu.SemaphoreType.DMA((planes * rows // ROWS,))],
        mine, other, local, row_back, jnp.asarray(depth_synthesis(pencils, False)),
        out_specs=HBM,
    )
    return grad_field, grad_weight


def solution(mesh):
    return jax.shard_map(
        on_device,
        mesh=mesh,
        in_specs=(P(None, "slab", "yz", None), P(None, None, None, ("slab", "yz")), P()),
        out_specs=(P(None, "slab", "yz", None), P(None, None, None, ("slab", "yz"))),
        check_vma=False,
    )
```

```python
import math

import jax
import jax.numpy as jnp
import ml_dtypes
import numpy as np
from jax import lax
from jax.experimental import pallas as pl
from jax.experimental.pallas import tpu as pltpu
from jax.sharding import PartitionSpec as P

KX = 16
KY = 16
MZ = 32
NY = 256
NZ = 256
ROWS = 8
LANES = 128
PIECES = 2
OUTER = 4

GELU_SCALE = 0.7978845608028654
GELU_CUBIC = 0.044715
BF16 = ml_dtypes.bfloat16
LARGE = 54272


def freqs(number, length):
    index = np.arange(number)
    return np.where(index < number // 2, index, length - number + index)


def angles(positions, frequencies, length):
    phase = (positions[:, None].astype(np.int64) * frequencies[None, :]) % length
    return phase * (2.0 * math.pi / length)


def halves(matrix):
    matrix = np.asarray(matrix, np.float32)
    upper = matrix.astype(BF16)
    lower = (matrix - upper.astype(np.float32)).astype(BF16)
    return upper, lower


def depth_freqs(pencils):
    groups = MZ // pencils
    return np.array([[g * pencils + q for g in range(groups)] for q in range(pencils)])


def depth_analysis(pencils, doubled):
    kz = depth_freqs(pencils)
    theta = angles(kz.reshape(-1), np.arange(NZ), NZ).reshape(pencils, -1, NZ)
    weight = np.where(kz == 0, 1.0, 2.0 if doubled else 1.0)[:, :, None]
    table = np.stack([np.cos(theta) * weight, -np.sin(theta) * weight], axis=1)
    return np.concatenate(halves(table.reshape(2 * MZ, NZ)), axis=0)


def depth_synthesis(pencils, doubled):
    kz = depth_freqs(pencils)
    theta = angles(kz.reshape(-1), np.arange(NZ), NZ).reshape(pencils, -1, NZ)
    weight = np.where(kz == 0, 1.0, 2.0 if doubled else 1.0)[:, :, None]
    table = np.stack([np.cos(theta) * weight, -np.sin(theta) * weight], axis=1)
    return np.tile(table.reshape(2 * MZ, NZ), (2, 1)).astype(BF16)


def row_analysis(pencils, planes):
    rows = NY // pencils
    tables = []
    for member in range(pencils):
        theta = angles(freqs(KY, NY), member * rows + np.arange(rows), NY)
        table = np.zeros((KY, 2, planes, 2, planes, rows))
        for x in range(planes):
            table[:, 0, x, 0, x] = np.cos(theta)
            table[:, 0, x, 1, x] = np.sin(theta)
            table[:, 1, x, 0, x] = -np.sin(theta)
            table[:, 1, x, 1, x] = np.cos(theta)
        table = table.reshape(KY * 2 * planes, 2 * planes * rows)
        tables.append(np.concatenate(halves(table), axis=0))
    return np.stack(tables)


def row_synthesis(pencils, planes):
    rows = NY // pencils
    tables = []
    for member in range(pencils):
        theta = angles(freqs(KY, NY), member * rows + np.arange(rows), NY)
        table = np.zeros((KY, 2, planes, 2, planes, rows))
        for x in range(planes):
            table[:, 0, x, 0, x] = np.cos(theta)
            table[:, 1, x, 0, x] = -np.sin(theta)
            table[:, 0, x, 1, x] = np.sin(theta)
            table[:, 1, x, 1, x] = np.cos(theta)
        upper, lower = halves(table.reshape(KY * 2 * planes, 2 * planes * rows))
        tables.append(np.concatenate([upper, upper, lower], axis=0))
    return np.stack(tables)


def member_tables(pencils, planes):
    depth = depth_analysis(pencils, False)
    ahead = row_analysis(pencils, planes)
    back = row_synthesis(pencils, planes)
    return np.stack([np.concatenate([depth, ahead[q], back[q]], 0) for q in range(pencils)])


def padded(table):
    return np.pad(table, ((0, 0), (0, max(0, LANES - table.shape[1]))))


def plane_analysis(slabs, planes, kyn, scale):
    theta = angles(np.arange(slabs * planes), freqs(KX, slabs * planes), slabs * planes)
    theta = theta.reshape(slabs, planes, KX)
    table = np.zeros((slabs, kyn, 2, planes, 2, kyn, KX))
    for k in range(kyn):
        table[:, k, 0, :, 0, k] = np.cos(theta)
        table[:, k, 1, :, 0, k] = np.sin(theta)
        table[:, k, 0, :, 1, k] = -np.sin(theta)
        table[:, k, 1, :, 1, k] = np.cos(theta)
    table = scale * table.reshape(slabs * kyn * 2 * planes, 2 * kyn * KX)
    upper, lower = halves(padded(table))
    return np.concatenate([upper, upper, lower], axis=0)


def plane_synthesis(slabs, planes, kyn, scale):
    theta = angles(np.arange(slabs * planes), freqs(KX, slabs * planes), slabs * planes)
    theta = theta.reshape(slabs, planes, KX)
    table = np.zeros((slabs, kyn, 2, planes, 2, kyn, KX))
    for k in range(kyn):
        table[:, k, 0, :, 0, k] = np.cos(theta)
        table[:, k, 0, :, 1, k] = -np.sin(theta)
        table[:, k, 1, :, 0, k] = np.sin(theta)
        table[:, k, 1, :, 1, k] = np.cos(theta)
    table = scale * table.reshape(slabs * kyn * 2 * planes, 2 * kyn * KX)
    return np.stack(halves(padded(table)))


def split(value):
    upper = value.astype(jnp.bfloat16)
    return upper, (value - upper.astype(jnp.float32)).astype(jnp.bfloat16)


def dot(left, right, left_dim=1, right_dim=0):
    return lax.dot_general(
        left, right, (((left_dim,), (right_dim,)), ((), ())), preferred_element_type=jnp.float32
    )


def analyze_depth(c, block, depth_ref, upper_ref, lower_ref):
    pencils, _, width = upper_ref.shape
    width = width // 2
    groups = MZ // pencils
    depth = dot(depth_ref[...], block, 1, 1)
    depth = depth[: 2 * MZ] + depth[2 * MZ :]
    for q in range(pencils):
        base = q * 2 * groups
        lines = [
            jnp.concatenate(
                [
                    depth[base : base + groups, e * width : (e + 1) * width],
                    depth[base + groups : base + 2 * groups, e * width : (e + 1) * width],
                ],
                axis=1,
            )
            for e in range(2)
        ]
        upper, lower = split(jnp.concatenate(lines, axis=0))
        upper_ref[q, c * groups : (c + 2) * groups] = upper
        lower_ref[q, c * groups : (c + 2) * groups] = lower


def analyze_rows(row_ref, upper_ref, lower_ref, kept_ref, sent_ref):
    blocks, pencils, line, half = kept_ref.shape
    count = row_ref.shape[0] // 2
    first = lax.axis_index("yz") % 2 == 0
    for q in range(pencils):
        both = dot(row_ref[...], upper_ref[q], 1, 1)
        total = both[:count] + both[count:] + dot(row_ref[:count], lower_ref[q], 1, 1)
        low = total[:, :half].reshape(blocks, line, half)
        high = total[:, half:].reshape(blocks, line, half)
        kept_ref[:, q] = jnp.where(first, low, high)
        sent_ref[:, q] = jnp.where(first, high, low)


def fetch(hbm, ref, sem):
    copy = pltpu.make_async_copy(hbm, ref, sem)
    copy.start()
    return copy


def analyze_kernel(
    grid_hbm, table_hbm, kept_ref, sent_ref, row_ref, lift_ref,
    grid_ref, depth_ref, upper_ref, lower_ref, piece_sem, table_sem,
):
    channels, planes, rows, cells = grid_hbm.shape
    step = channels // PIECES
    table = table_hbm.at[lax.axis_index("yz")]
    first = depth_ref.shape[0]
    second = first + row_ref.shape[0]
    depth_copy = fetch(table.at[pl.ds(0, first)], depth_ref, table_sem.at[0])
    pieces = [
        fetch(grid_hbm.at[pl.ds(i * step, step)], grid_ref.at[pl.ds(i * step, step)], piece_sem.at[i])
        for i in range(PIECES)
    ]
    row_copy = fetch(table.at[pl.ds(first, row_ref.shape[0])], row_ref, table_sem.at[1])
    lift_copy = fetch(table.at[pl.ds(second, lift_ref.shape[0])], lift_ref, table_sem.at[2])
    depth_copy.wait()
    for c in range(0, channels, 2):
        if c % step == 0:
            pieces[c // step].wait()
        block = grid_ref[c : c + 2].reshape(2 * planes * rows, cells)
        analyze_depth(c, block, depth_ref, upper_ref, lower_ref)
    row_copy.wait()
    analyze_rows(row_ref, upper_ref, lower_ref, kept_ref, sent_ref)
    lift_copy.wait()


def collect(sums_ref, plane_ref, turn_ref, kyn, channels):
    slabs, pencils, line, half = sums_ref.shape
    sides = []
    for core in range(2):
        side = sums_ref[:, core]
        for member in range(core + 2, pencils, 2):
            side = side + sums_ref[:, member]
        sides.append(side.reshape(slabs * line, half))
    upper, lower = split(jnp.concatenate(sides, axis=1))
    turn_ref[...] = dot(jnp.concatenate([upper, lower, upper], axis=0), plane_ref[...], 0, 0)
    groups = 2 * half // channels
    lines = [turn_ref[pl.ds(g, channels, stride=groups)] for g in range(groups)]
    parts = []
    for part in range(2):
        pieces = []
        for k in range(kyn):
            start = (part * kyn + k) * KX
            pieces += [line[:, start : start + KX] for line in lines]
        parts.append(jnp.concatenate(pieces, axis=1) if len(pieces) > 1 else pieces[0])
    return parts


def distribute(real, imag, plane_ref, turn_ref, kyn, out_ref):
    slabs, pencils, line, half = out_ref.shape
    channels = real.shape[0]
    groups = 2 * half // channels
    for g in range(groups):
        pieces = []
        for value in (real, imag):
            for k in range(kyn):
                start = (k * groups + g) * KX
                pieces.append(value[:, start : start + KX])
        rest = turn_ref.shape[1] - 2 * kyn * KX
        if rest:
            pieces.append(jnp.zeros((channels, rest), jnp.float32))
        turn_ref[pl.ds(g, channels, stride=groups)] = jnp.concatenate(pieces, axis=1)
    upper, lower = split(turn_ref[...])
    total = (
        dot(plane_ref[0], upper, 1, 1)
        + dot(plane_ref[1], upper, 1, 1)
        + dot(plane_ref[0], lower, 1, 1)
    )
    for member in range(pencils):
        side = total[:, member % 2 * half : (member % 2 + 1) * half]
        out_ref[:, member] = side.reshape(slabs, line, half)


def mix_kernel(
    kyn, sums_ref, weight_ref, ahead_ref, back_ref, out_ref, coef_hbm, coef_ref, mixed_ref, turn_ref, sem
):
    real, imag = collect(sums_ref, ahead_ref, turn_ref, kyn, weight_ref.shape[1])
    coef_ref[0] = real
    coef_ref[1] = imag
    copy = fetch(coef_ref, coef_hbm, sem)
    for o in range(weight_ref.shape[1]):
        weight_real = weight_ref[0, o].astype(jnp.float32)
        weight_imag = weight_ref[1, o].astype(jnp.float32)
        mixed_ref[0, o : o + 1] = jnp.sum(
            weight_real * real - weight_imag * imag, axis=0, keepdims=True
        )
        mixed_ref[1, o : o + 1] = jnp.sum(
            weight_real * imag + weight_imag * real, axis=0, keepdims=True
        )
    distribute(mixed_ref[0], mixed_ref[1], back_ref, turn_ref, kyn, out_ref)
    copy.wait()


def unmix_kernel(kyn, sums_ref, weight_ref, ahead_ref, back_ref, out_ref, coef_ref, turn_ref):
    real, imag = collect(sums_ref, ahead_ref, turn_ref, kyn, weight_ref.shape[1])
    coef_ref[0] = real
    coef_ref[1] = imag
    modes_real = jnp.zeros_like(real)
    modes_imag = jnp.zeros_like(real)
    for o in range(weight_ref.shape[1]):
        weight_real = weight_ref[0, o].astype(jnp.float32)
        weight_imag = weight_ref[1, o].astype(jnp.float32)
        back_real = coef_ref[0, o : o + 1]
        back_imag = coef_ref[1, o : o + 1]
        modes_real = modes_real + (weight_real * back_real + weight_imag * back_imag)
        modes_imag = modes_imag + (weight_real * back_imag - weight_imag * back_real)
    distribute(modes_real, modes_imag, back_ref, turn_ref, kyn, out_ref)


def outer_kernel(coef_ref, back_ref, out_hbm, out_ref, sems):
    real, imag = coef_ref[0], coef_ref[1]
    channels = back_ref.shape[1]
    step = channels // OUTER
    copies = []
    for o in range(channels):
        back_real = back_ref[0, o : o + 1]
        back_imag = back_ref[1, o : o + 1]
        out_ref[0, o] = back_real * real + back_imag * imag
        out_ref[1, o] = back_imag * real - back_real * imag
        if (o + 1) % step == 0:
            start = o + 1 - step
            for part in range(2):
                copies.append(
                    fetch(
                        out_ref.at[part, pl.ds(start, step)],
                        out_hbm.at[part, pl.ds(start, step)],
                        sems.at[len(copies)],
                    )
                )
    for copy in copies:
        copy.wait()


def lift(mine_ref, other_ref, row_ref):
    blocks, pencils, line, half = mine_ref.shape
    first = lax.axis_index("yz") % 2 == 0
    lines = []
    for q in range(pencils):
        mine = mine_ref[:, q].reshape(blocks * line, half)
        other = other_ref[:, q].reshape(blocks * line, half)
        value = jnp.concatenate(
            [jnp.where(first, mine, other), jnp.where(first, other, mine)], axis=1
        )
        upper, lower = split(value)
        stacked = jnp.concatenate([upper, lower, upper], axis=0)
        lines.append(dot(stacked, row_ref[...], 0, 0))
    return lines


def spread(lines, o):
    groups = MZ // len(lines)
    lanes = lines[0].shape[1] // 2
    block = jnp.concatenate(
        [
            line[o * groups : (o + 1) * groups, part * lanes : (part + 1) * lanes]
            for line in lines
            for part in range(2)
        ],
        axis=0,
    )
    upper = block.astype(jnp.bfloat16).astype(jnp.float32)
    return jnp.concatenate([upper, block - upper], axis=0).T.astype(jnp.bfloat16)


def local_kernel(grid_ref, wide_ref, out_ref):
    channels, planes, rows, cells = grid_ref.shape
    for x in range(planes):
        for y in range(0, rows, 2 * ROWS):
            block = grid_ref[:, x, y : y + 2 * ROWS]
            for start in (0, ROWS):
                part = block[:, start : start + ROWS].reshape(channels * ROWS, cells)
                total = dot(wide_ref[...], part).reshape(channels, ROWS, cells)
                out_ref[:, x, y + start : y + start + ROWS] = total


def middle_kernel(
    mine_ref, other_ref, local_ref, lift_ref, synth_ref, depth_ref, row_ref,
    up_ref, kept_ref, sent_ref, upper_ref, lower_ref,
):
    channels, planes, rows, cells = local_ref.shape
    lines = lift(mine_ref, other_ref, lift_ref)
    for o in range(0, channels, 2):
        blocks = []
        for e in range(o, o + 2):
            before = dot(spread(lines, e), synth_ref[...])
            before = before + local_ref[e].reshape(planes * rows, cells)
            square = before * before
            tangent = jnp.tanh(before * (GELU_SCALE + (GELU_SCALE * GELU_CUBIC) * square))
            above = 1.0 + tangent
            below = 1.0 - tangent
            quarter = 0.25 * GELU_SCALE + (0.75 * GELU_SCALE * GELU_CUBIC) * square
            upstream = (before * (above * above)) * (0.25 + (before * below) * quarter)
            blocks.append(upstream.astype(jnp.bfloat16))
            up_ref[e] = blocks[-1].reshape(planes, rows, cells)
        analyze_depth(o, jnp.concatenate(blocks, axis=0), depth_ref, upper_ref, lower_ref)
    analyze_rows(row_ref, upper_ref, lower_ref, kept_ref, sent_ref)


def final_kernel(
    mine_ref, other_ref, local_ref, lift_ref, synth_ref, out_hbm, result_ref, out_sems
):
    channels, planes, rows, cells = local_ref.shape
    lines = lift(mine_ref, other_ref, lift_ref)
    step = channels // OUTER
    copies = []
    for o in range(channels):
        total = dot(spread(lines, o), synth_ref[...])
        total = total + local_ref[o].reshape(planes * rows, cells)
        result_ref[o] = total.astype(jnp.bfloat16).reshape(planes, rows, cells)
        if (o + 1) % step == 0:
            part = pl.ds(o + 1 - step, step)
            copies.append(fetch(result_ref.at[part], out_hbm.at[part], out_sems.at[len(copies)]))
    for copy in copies:
        copy.wait()


VMEM = pl.BlockSpec(memory_space=pltpu.VMEM)
HBM = pl.BlockSpec(memory_space=pltpu.HBM)


def call(kernel, outs, scratch, *operands, far=(), out_specs=None, limit=20480):
    return pl.pallas_call(
        kernel,
        out_shape=outs,
        in_specs=[HBM if i in far else VMEM for i in range(len(operands))],
        out_specs=jax.tree.map(lambda _: VMEM, outs) if out_specs is None else out_specs,
        scratch_shapes=scratch,
        compiler_params=pltpu.CompilerParams(vmem_limit_bytes=limit << 10),
        cost_estimate=pl.CostEstimate(flops=1 << 30, bytes_accessed=4 << 20, transcendentals=0),
    )(*operands)


def f32(*shape):
    return jax.ShapeDtypeStruct(shape, jnp.float32)


def bf16(*shape):
    return jax.ShapeDtypeStruct(shape, jnp.bfloat16)


def on_device(grid_field, spectral_weight, local_weight):
    channels, planes, rows, cells = grid_field.shape
    slabs = lax.axis_size("slab")
    pencils = lax.axis_size("yz")
    groups = MZ // pencils
    scale = 1.0 / math.sqrt(planes * slabs * NY * NZ)
    pairs = KY * groups // slabs
    kyn = max(1, pairs // groups)
    gn = pairs // kyn
    blocks = KY // kyn
    turns = groups // gn
    half = channels // 2
    line = kyn * 2 * planes
    modes = spectral_weight.shape[3]

    table = jnp.asarray(member_tables(pencils, planes))
    plane_ahead = jnp.asarray(plane_analysis(slabs, planes, kyn, scale))
    plane_back = jnp.asarray(plane_synthesis(slabs, planes, kyn, scale))
    repeat = jnp.asarray(np.repeat(np.eye(channels), ROWS, axis=0).astype(BF16))
    mask = jnp.asarray(np.tile(np.eye(ROWS), (channels, channels)).astype(BF16))
    neighbours = [(i, i ^ 1) for i in range(pencils)]

    def widen(weight):
        rows_wide = dot(repeat, weight).astype(jnp.bfloat16)
        return dot(rows_wide, repeat, 1, 1).astype(jnp.bfloat16) * mask

    def to_owner(kept, sent, beside):
        given = lax.ppermute(sent, "yz", neighbours)
        given, beside = lax.optimization_barrier((given, beside))
        parts = kept + given
        if turns > 1:
            parts = parts.reshape(blocks, pencils, line, half, turns, gn)
            parts = jnp.transpose(parts, (0, 4, 1, 2, 3, 5))
        parts = parts.reshape(slabs * pencils, line, half * gn)
        moved = lax.all_to_all(parts, ("slab", "yz"), 0, 0, tiled=True)
        return moved.reshape(slabs, pencils, line, half * gn), beside

    def from_owner(values, work):
        values = values.reshape(slabs * pencils, line, half * gn)
        moved = lax.all_to_all(values, ("slab", "yz"), 0, 0, tiled=True)
        if turns > 1:
            moved = moved.reshape(blocks, turns, pencils, line, half, gn)
            moved = jnp.transpose(moved, (0, 2, 3, 4, 1, 5))
        moved = moved.reshape(blocks, pencils, line, half * groups)
        other = lax.ppermute(moved, "yz", neighbours)
        if work is None:
            return moved, other, None
        return lax.optimization_barrier((moved, other, work(moved)))

    halves_scratch = [pltpu.VMEM((pencils, channels * groups, 2 * planes * rows), jnp.bfloat16)] * 2
    turn_scratch = pltpu.VMEM((channels * gn, plane_ahead.shape[1]), jnp.float32)
    field_scratch = pltpu.VMEM(grid_field.shape, jnp.bfloat16)
    sums = f32(blocks, pencils, line, half * groups)
    given = f32(slabs, pencils, line, half * gn)
    coefs = f32(2, channels, modes)
    values_count = KY * 2 * planes

    kept, sent, row_ahead, row_back = call(
        analyze_kernel, (sums, sums, bf16(2 * values_count, 2 * planes * rows), bf16(3 * values_count, 2 * planes * rows)),
        [
            field_scratch, pltpu.VMEM((4 * MZ, NZ), jnp.bfloat16), *halves_scratch,
            pltpu.SemaphoreType.DMA((PIECES,)), pltpu.SemaphoreType.DMA((3,)),
        ],
        grid_field, table, far=(0, 1), limit=LARGE,
    )
    received, (wide, wide_back) = to_owner(
        kept, sent, (widen(local_weight), widen(local_weight.T))
    )

    def mix(*refs):
        mix_kernel(kyn, *refs)

    values, coef = call(
        mix, (given, coefs),
        [pltpu.VMEM((2, channels, modes), jnp.float32)] * 2 + [turn_scratch, pltpu.SemaphoreType.DMA],
        received, spectral_weight, plane_ahead, plane_back, out_specs=(VMEM, HBM),
    )
    def local_ahead(moved):
        _, late = lax.optimization_barrier((moved, wide))
        return call(local_kernel, f32(*grid_field.shape), [], grid_field, late)

    mine, other, local = from_owner(values, local_ahead)
    upstream, kept, sent = call(
        middle_kernel, (bf16(*grid_field.shape), sums, sums),
        halves_scratch,
        mine, other, local, row_back,
        jnp.asarray(depth_synthesis(pencils, True)), jnp.asarray(depth_analysis(pencils, True)), row_ahead,
    )
    received, local = to_owner(
        kept, sent, call(local_kernel, f32(*grid_field.shape), [], upstream, wide_back)
    )

    def unmix(*refs):
        unmix_kernel(kyn, *refs)

    values, back = call(
        unmix, (given, coefs), [turn_scratch],
        received, spectral_weight, plane_ahead, plane_back,
    )

    def outer(moved):
        _, late = lax.optimization_barrier((moved, back))
        return call(
            outer_kernel, f32(2, channels, channels, modes),
            [
                pltpu.VMEM((2, channels, channels, modes), jnp.float32),
                pltpu.SemaphoreType.DMA((2 * OUTER,)),
            ],
            coef, late, out_specs=HBM,
        )

    mine, other, grad_weight = from_owner(values, outer)
    grad_field = call(
        final_kernel, bf16(*grid_field.shape),
        [field_scratch, pltpu.SemaphoreType.DMA((OUTER,))],
        mine, other, local, row_back, jnp.asarray(depth_synthesis(pencils, False)),
        out_specs=HBM,
    )
    return grad_field, grad_weight


def solution(mesh):
    return jax.shard_map(
        on_device,
        mesh=mesh,
        in_specs=(P(None, "slab", "yz", None), P(None, None, None, ("slab", "yz")), P()),
        out_specs=(P(None, "slab", "yz", None), P(None, None, None, ("slab", "yz"))),
        check_vma=False,
    )
```

```python
import math

import jax
import jax.numpy as jnp
import ml_dtypes
import numpy as np
from jax import lax
from jax.experimental import pallas as pl
from jax.experimental.pallas import tpu as pltpu
from jax.sharding import PartitionSpec as P

KX = 16
KY = 16
MZ = 32
NY = 256
NZ = 256
ROWS = 8
LANES = 128
PIECES = 2
OUTER = 4

GELU_SCALE = 0.7978845608028654
GELU_CUBIC = 0.044715
BF16 = ml_dtypes.bfloat16
LARGE = 54272


def freqs(number, length):
    index = np.arange(number)
    return np.where(index < number // 2, index, length - number + index)


def angles(positions, frequencies, length):
    phase = (positions[:, None].astype(np.int64) * frequencies[None, :]) % length
    return phase * (2.0 * math.pi / length)


def halves(matrix):
    matrix = np.asarray(matrix, np.float32)
    upper = matrix.astype(BF16)
    lower = (matrix - upper.astype(np.float32)).astype(BF16)
    return upper, lower


def depth_freqs(pencils):
    groups = MZ // pencils
    return np.array([[g * pencils + q for g in range(groups)] for q in range(pencils)])


def depth_analysis(pencils, doubled):
    kz = depth_freqs(pencils)
    theta = angles(kz.reshape(-1), np.arange(NZ), NZ).reshape(pencils, -1, NZ)
    weight = np.where(kz == 0, 1.0, 2.0 if doubled else 1.0)[:, :, None]
    table = np.stack([np.cos(theta) * weight, -np.sin(theta) * weight], axis=1)
    return np.concatenate(halves(table.reshape(2 * MZ, NZ)), axis=0)


def depth_synthesis(pencils, doubled):
    kz = depth_freqs(pencils)
    theta = angles(kz.reshape(-1), np.arange(NZ), NZ).reshape(pencils, -1, NZ)
    weight = np.where(kz == 0, 1.0, 2.0 if doubled else 1.0)[:, :, None]
    table = np.stack([np.cos(theta) * weight, -np.sin(theta) * weight], axis=1)
    return np.tile(table.reshape(2 * MZ, NZ), (2, 1)).astype(BF16)


def row_analysis(pencils, planes):
    rows = NY // pencils
    tables = []
    for member in range(pencils):
        theta = angles(freqs(KY, NY), member * rows + np.arange(rows), NY)
        table = np.zeros((KY, 2, planes, 2, planes, rows))
        for x in range(planes):
            table[:, 0, x, 0, x] = np.cos(theta)
            table[:, 0, x, 1, x] = np.sin(theta)
            table[:, 1, x, 0, x] = -np.sin(theta)
            table[:, 1, x, 1, x] = np.cos(theta)
        table = table.reshape(KY * 2 * planes, 2 * planes * rows)
        tables.append(np.concatenate(halves(table), axis=0))
    return np.stack(tables)


def row_synthesis(pencils, planes):
    rows = NY // pencils
    tables = []
    for member in range(pencils):
        theta = angles(freqs(KY, NY), member * rows + np.arange(rows), NY)
        table = np.zeros((KY, 2, planes, 2, planes, rows))
        for x in range(planes):
            table[:, 0, x, 0, x] = np.cos(theta)
            table[:, 1, x, 0, x] = -np.sin(theta)
            table[:, 0, x, 1, x] = np.sin(theta)
            table[:, 1, x, 1, x] = np.cos(theta)
        upper, lower = halves(table.reshape(KY * 2 * planes, 2 * planes * rows))
        tables.append(np.concatenate([upper, upper, lower], axis=0))
    return np.stack(tables)


def member_tables(pencils, planes):
    depth = depth_analysis(pencils, False)
    ahead = row_analysis(pencils, planes)
    back = row_synthesis(pencils, planes)
    return np.stack([np.concatenate([depth, ahead[q], back[q]], 0) for q in range(pencils)])


def padded(table):
    return np.pad(table, ((0, 0), (0, max(0, LANES - table.shape[1]))))


def plane_analysis(slabs, planes, kyn, scale):
    theta = angles(np.arange(slabs * planes), freqs(KX, slabs * planes), slabs * planes)
    theta = theta.reshape(slabs, planes, KX)
    table = np.zeros((slabs, kyn, 2, planes, 2, kyn, KX))
    for k in range(kyn):
        table[:, k, 0, :, 0, k] = np.cos(theta)
        table[:, k, 1, :, 0, k] = np.sin(theta)
        table[:, k, 0, :, 1, k] = -np.sin(theta)
        table[:, k, 1, :, 1, k] = np.cos(theta)
    table = scale * table.reshape(slabs * kyn * 2 * planes, 2 * kyn * KX)
    upper, lower = halves(padded(table))
    return np.concatenate([upper, upper, lower], axis=0)


def plane_synthesis(slabs, planes, kyn, scale):
    theta = angles(np.arange(slabs * planes), freqs(KX, slabs * planes), slabs * planes)
    theta = theta.reshape(slabs, planes, KX)
    table = np.zeros((slabs, kyn, 2, planes, 2, kyn, KX))
    for k in range(kyn):
        table[:, k, 0, :, 0, k] = np.cos(theta)
        table[:, k, 0, :, 1, k] = -np.sin(theta)
        table[:, k, 1, :, 0, k] = np.sin(theta)
        table[:, k, 1, :, 1, k] = np.cos(theta)
    table = scale * table.reshape(slabs * kyn * 2 * planes, 2 * kyn * KX)
    return np.stack(halves(padded(table)))


def split(value):
    upper = value.astype(jnp.bfloat16)
    return upper, (value - upper.astype(jnp.float32)).astype(jnp.bfloat16)


def dot(left, right, left_dim=1, right_dim=0):
    return lax.dot_general(
        left, right, (((left_dim,), (right_dim,)), ((), ())), preferred_element_type=jnp.float32
    )


def analyze_depth(c, block, depth_ref, upper_ref, lower_ref):
    pencils, _, width = upper_ref.shape
    width = width // 2
    groups = MZ // pencils
    depth = dot(depth_ref[...], block, 1, 1)
    depth = depth[: 2 * MZ] + depth[2 * MZ :]
    for q in range(pencils):
        base = q * 2 * groups
        lines = [
            jnp.concatenate(
                [
                    depth[base : base + groups, e * width : (e + 1) * width],
                    depth[base + groups : base + 2 * groups, e * width : (e + 1) * width],
                ],
                axis=1,
            )
            for e in range(2)
        ]
        upper, lower = split(jnp.concatenate(lines, axis=0))
        upper_ref[q, c * groups : (c + 2) * groups] = upper
        lower_ref[q, c * groups : (c + 2) * groups] = lower


def analyze_rows(row_ref, upper_ref, lower_ref, kept_ref, sent_ref):
    blocks, pencils, line, half = kept_ref.shape
    count = row_ref.shape[0] // 2
    first = lax.axis_index("yz") % 2 == 0
    for q in range(pencils):
        both = dot(row_ref[...], upper_ref[q], 1, 1)
        total = both[:count] + both[count:] + dot(row_ref[:count], lower_ref[q], 1, 1)
        low = total[:, :half].reshape(blocks, line, half)
        high = total[:, half:].reshape(blocks, line, half)
        kept_ref[:, q] = jnp.where(first, low, high)
        sent_ref[:, q] = jnp.where(first, high, low)


def fetch(hbm, ref, sem, lane=0):
    copy = pltpu.make_async_copy(hbm, ref, sem)
    copy.start(priority=lane)
    return copy


def analyze_kernel(
    grid_hbm, table_hbm, kept_ref, sent_ref, row_ref, lift_ref,
    grid_ref, depth_ref, upper_ref, lower_ref, piece_sem, table_sem,
):
    channels, planes, rows, cells = grid_hbm.shape
    step = channels // PIECES
    table = table_hbm.at[lax.axis_index("yz")]
    first = depth_ref.shape[0]
    second = first + row_ref.shape[0]
    depth_copy = fetch(table.at[pl.ds(0, first)], depth_ref, table_sem.at[0])
    pieces = [
        fetch(grid_hbm.at[pl.ds(i * step, step)], grid_ref.at[pl.ds(i * step, step)], piece_sem.at[i], i % 2)
        for i in range(PIECES)
    ]
    row_copy = fetch(table.at[pl.ds(first, row_ref.shape[0])], row_ref, table_sem.at[1])
    lift_copy = fetch(table.at[pl.ds(second, lift_ref.shape[0])], lift_ref, table_sem.at[2])
    depth_copy.wait()
    for c in range(0, channels, 2):
        if c % step == 0:
            pieces[c // step].wait()
        block = grid_ref[c : c + 2].reshape(2 * planes * rows, cells)
        analyze_depth(c, block, depth_ref, upper_ref, lower_ref)
    row_copy.wait()
    analyze_rows(row_ref, upper_ref, lower_ref, kept_ref, sent_ref)
    lift_copy.wait()


def collect(sums_ref, plane_ref, turn_ref, kyn, channels):
    slabs, pencils, line, half = sums_ref.shape
    sides = []
    for core in range(2):
        side = sums_ref[:, core]
        for member in range(core + 2, pencils, 2):
            side = side + sums_ref[:, member]
        sides.append(side.reshape(slabs * line, half))
    upper, lower = split(jnp.concatenate(sides, axis=1))
    turn_ref[...] = dot(jnp.concatenate([upper, lower, upper], axis=0), plane_ref[...], 0, 0)
    groups = 2 * half // channels
    lines = [turn_ref[pl.ds(g, channels, stride=groups)] for g in range(groups)]
    parts = []
    for part in range(2):
        pieces = []
        for k in range(kyn):
            start = (part * kyn + k) * KX
            pieces += [line[:, start : start + KX] for line in lines]
        parts.append(jnp.concatenate(pieces, axis=1) if len(pieces) > 1 else pieces[0])
    return parts


def distribute(real, imag, plane_ref, turn_ref, kyn, out_ref):
    slabs, pencils, line, half = out_ref.shape
    channels = real.shape[0]
    groups = 2 * half // channels
    for g in range(groups):
        pieces = []
        for value in (real, imag):
            for k in range(kyn):
                start = (k * groups + g) * KX
                pieces.append(value[:, start : start + KX])
        rest = turn_ref.shape[1] - 2 * kyn * KX
        if rest:
            pieces.append(jnp.zeros((channels, rest), jnp.float32))
        turn_ref[pl.ds(g, channels, stride=groups)] = jnp.concatenate(pieces, axis=1)
    upper, lower = split(turn_ref[...])
    total = (
        dot(plane_ref[0], upper, 1, 1)
        + dot(plane_ref[1], upper, 1, 1)
        + dot(plane_ref[0], lower, 1, 1)
    )
    for member in range(pencils):
        side = total[:, member % 2 * half : (member % 2 + 1) * half]
        out_ref[:, member] = side.reshape(slabs, line, half)


def mix_kernel(
    kyn, sums_ref, weight_ref, ahead_ref, back_ref, out_ref, coef_hbm, coef_ref, mixed_ref, turn_ref, sem
):
    real, imag = collect(sums_ref, ahead_ref, turn_ref, kyn, weight_ref.shape[1])
    coef_ref[0] = real
    coef_ref[1] = imag
    copy = fetch(coef_ref, coef_hbm, sem)
    for o in range(weight_ref.shape[1]):
        weight_real = weight_ref[0, o].astype(jnp.float32)
        weight_imag = weight_ref[1, o].astype(jnp.float32)
        mixed_ref[0, o : o + 1] = jnp.sum(
            weight_real * real - weight_imag * imag, axis=0, keepdims=True
        )
        mixed_ref[1, o : o + 1] = jnp.sum(
            weight_real * imag + weight_imag * real, axis=0, keepdims=True
        )
    distribute(mixed_ref[0], mixed_ref[1], back_ref, turn_ref, kyn, out_ref)
    copy.wait()


def unmix_kernel(kyn, sums_ref, weight_ref, ahead_ref, back_ref, out_ref, coef_ref, turn_ref):
    real, imag = collect(sums_ref, ahead_ref, turn_ref, kyn, weight_ref.shape[1])
    coef_ref[0] = real
    coef_ref[1] = imag
    modes_real = jnp.zeros_like(real)
    modes_imag = jnp.zeros_like(real)
    for o in range(weight_ref.shape[1]):
        weight_real = weight_ref[0, o].astype(jnp.float32)
        weight_imag = weight_ref[1, o].astype(jnp.float32)
        back_real = coef_ref[0, o : o + 1]
        back_imag = coef_ref[1, o : o + 1]
        modes_real = modes_real + (weight_real * back_real + weight_imag * back_imag)
        modes_imag = modes_imag + (weight_real * back_imag - weight_imag * back_real)
    distribute(modes_real, modes_imag, back_ref, turn_ref, kyn, out_ref)


def outer_kernel(coef_ref, back_ref, out_ref):
    real, imag = coef_ref[0], coef_ref[1]
    for o in range(back_ref.shape[1]):
        back_real = back_ref[0, o : o + 1]
        back_imag = back_ref[1, o : o + 1]
        out_ref[0, o] = back_real * real + back_imag * imag
        out_ref[1, o] = back_imag * real - back_real * imag


def lift(mine_ref, other_ref, row_ref):
    blocks, pencils, line, half = mine_ref.shape
    first = lax.axis_index("yz") % 2 == 0
    lines = []
    for q in range(pencils):
        mine = mine_ref[:, q].reshape(blocks * line, half)
        other = other_ref[:, q].reshape(blocks * line, half)
        value = jnp.concatenate(
            [jnp.where(first, mine, other), jnp.where(first, other, mine)], axis=1
        )
        upper, lower = split(value)
        stacked = jnp.concatenate([upper, lower, upper], axis=0)
        lines.append(dot(stacked, row_ref[...], 0, 0))
    return lines


def spread(lines, o):
    groups = MZ // len(lines)
    lanes = lines[0].shape[1] // 2
    block = jnp.concatenate(
        [
            line[o * groups : (o + 1) * groups, part * lanes : (part + 1) * lanes]
            for line in lines
            for part in range(2)
        ],
        axis=0,
    )
    upper = block.astype(jnp.bfloat16).astype(jnp.float32)
    return jnp.concatenate([upper, block - upper], axis=0).T.astype(jnp.bfloat16)


def local_kernel(grid_ref, wide_ref, out_ref):
    channels, planes, rows, cells = grid_ref.shape
    for x in range(planes):
        for y in range(0, rows, 2 * ROWS):
            block = grid_ref[:, x, y : y + 2 * ROWS]
            for start in (0, ROWS):
                part = block[:, start : start + ROWS].reshape(channels * ROWS, cells)
                total = dot(wide_ref[...], part).reshape(channels, ROWS, cells)
                out_ref[:, x, y + start : y + start + ROWS] = total


def middle_kernel(
    mine_ref, other_ref, local_ref, lift_ref, synth_ref, depth_ref, row_ref,
    up_ref, kept_ref, sent_ref, upper_ref, lower_ref,
):
    channels, planes, rows, cells = local_ref.shape
    lines = lift(mine_ref, other_ref, lift_ref)
    for o in range(0, channels, 2):
        blocks = []
        for e in range(o, o + 2):
            before = dot(spread(lines, e), synth_ref[...])
            before = before + local_ref[e].reshape(planes * rows, cells)
            square = before * before
            tangent = jnp.tanh(before * (GELU_SCALE + (GELU_SCALE * GELU_CUBIC) * square))
            above = 1.0 + tangent
            below = 1.0 - tangent
            quarter = 0.25 * GELU_SCALE + (0.75 * GELU_SCALE * GELU_CUBIC) * square
            upstream = (before * (above * above)) * (0.25 + (before * below) * quarter)
            blocks.append(upstream.astype(jnp.bfloat16))
            up_ref[e] = blocks[-1].reshape(planes, rows, cells)
        analyze_depth(o, jnp.concatenate(blocks, axis=0), depth_ref, upper_ref, lower_ref)
    analyze_rows(row_ref, upper_ref, lower_ref, kept_ref, sent_ref)


def final_kernel(
    mine_ref, other_ref, local_ref, lift_ref, synth_ref, product_ref, out_hbm, weight_hbm,
    result_ref, out_sems, weight_sem,
):
    channels, planes, rows, cells = local_ref.shape
    weight_copy = fetch(product_ref, weight_hbm, weight_sem, 1)
    lines = lift(mine_ref, other_ref, lift_ref)
    step = channels // OUTER
    copies = []
    for o in range(channels):
        total = dot(spread(lines, o), synth_ref[...])
        total = total + local_ref[o].reshape(planes * rows, cells)
        result_ref[o] = total.astype(jnp.bfloat16).reshape(planes, rows, cells)
        if (o + 1) % step == 0:
            part = pl.ds(o + 1 - step, step)
            copies.append(fetch(result_ref.at[part], out_hbm.at[part], out_sems.at[len(copies)]))
    for copy in [weight_copy] + copies:
        copy.wait()


VMEM = pl.BlockSpec(memory_space=pltpu.VMEM)
HBM = pl.BlockSpec(memory_space=pltpu.HBM)


def call(kernel, outs, scratch, *operands, far=(), out_specs=None, limit=20480):
    return pl.pallas_call(
        kernel,
        out_shape=outs,
        in_specs=[HBM if i in far else VMEM for i in range(len(operands))],
        out_specs=jax.tree.map(lambda _: VMEM, outs) if out_specs is None else out_specs,
        scratch_shapes=scratch,
        compiler_params=pltpu.CompilerParams(vmem_limit_bytes=limit << 10),
        cost_estimate=pl.CostEstimate(flops=1 << 30, bytes_accessed=4 << 20, transcendentals=0),
    )(*operands)


def f32(*shape):
    return jax.ShapeDtypeStruct(shape, jnp.float32)


def bf16(*shape):
    return jax.ShapeDtypeStruct(shape, jnp.bfloat16)


def on_device(grid_field, spectral_weight, local_weight):
    channels, planes, rows, cells = grid_field.shape
    slabs = lax.axis_size("slab")
    pencils = lax.axis_size("yz")
    groups = MZ // pencils
    scale = 1.0 / math.sqrt(planes * slabs * NY * NZ)
    pairs = KY * groups // slabs
    kyn = max(1, pairs // groups)
    gn = pairs // kyn
    blocks = KY // kyn
    turns = groups // gn
    half = channels // 2
    line = kyn * 2 * planes
    modes = spectral_weight.shape[3]

    table = jnp.asarray(member_tables(pencils, planes))
    plane_ahead = jnp.asarray(plane_analysis(slabs, planes, kyn, scale))
    plane_back = jnp.asarray(plane_synthesis(slabs, planes, kyn, scale))
    repeat = jnp.asarray(np.repeat(np.eye(channels), ROWS, axis=0).astype(BF16))
    mask = jnp.asarray(np.tile(np.eye(ROWS), (channels, channels)).astype(BF16))
    neighbours = [(i, i ^ 1) for i in range(pencils)]

    def widen(weight):
        rows_wide = dot(repeat, weight).astype(jnp.bfloat16)
        return dot(rows_wide, repeat, 1, 1).astype(jnp.bfloat16) * mask

    def to_owner(kept, sent, beside):
        given = lax.ppermute(sent, "yz", neighbours)
        given, beside = lax.optimization_barrier((given, beside))
        parts = kept + given
        if turns > 1:
            parts = parts.reshape(blocks, pencils, line, half, turns, gn)
            parts = jnp.transpose(parts, (0, 4, 1, 2, 3, 5))
        parts = parts.reshape(slabs * pencils, line, half * gn)
        moved = lax.all_to_all(parts, ("slab", "yz"), 0, 0, tiled=True)
        return moved.reshape(slabs, pencils, line, half * gn), beside

    def from_owner(values, work):
        values = values.reshape(slabs * pencils, line, half * gn)
        moved = lax.all_to_all(values, ("slab", "yz"), 0, 0, tiled=True)
        if turns > 1:
            moved = moved.reshape(blocks, turns, pencils, line, half, gn)
            moved = jnp.transpose(moved, (0, 2, 3, 4, 1, 5))
        moved = moved.reshape(blocks, pencils, line, half * groups)
        other = lax.ppermute(moved, "yz", neighbours)
        if work is None:
            return moved, other, None
        return lax.optimization_barrier((moved, other, work(moved)))

    halves_scratch = [pltpu.VMEM((pencils, channels * groups, 2 * planes * rows), jnp.bfloat16)] * 2
    turn_scratch = pltpu.VMEM((channels * gn, plane_ahead.shape[1]), jnp.float32)
    field_scratch = pltpu.VMEM(grid_field.shape, jnp.bfloat16)
    sums = f32(blocks, pencils, line, half * groups)
    given = f32(slabs, pencils, line, half * gn)
    coefs = f32(2, channels, modes)
    values_count = KY * 2 * planes

    kept, sent, row_ahead, row_back = call(
        analyze_kernel, (sums, sums, bf16(2 * values_count, 2 * planes * rows), bf16(3 * values_count, 2 * planes * rows)),
        [
            field_scratch, pltpu.VMEM((4 * MZ, NZ), jnp.bfloat16), *halves_scratch,
            pltpu.SemaphoreType.DMA((PIECES,)), pltpu.SemaphoreType.DMA((3,)),
        ],
        grid_field, table, far=(0, 1), limit=LARGE,
    )
    received, (wide, wide_back) = to_owner(
        kept, sent, (widen(local_weight), widen(local_weight.T))
    )

    def mix(*refs):
        mix_kernel(kyn, *refs)

    values, coef = call(
        mix, (given, coefs),
        [pltpu.VMEM((2, channels, modes), jnp.float32)] * 2 + [turn_scratch, pltpu.SemaphoreType.DMA],
        received, spectral_weight, plane_ahead, plane_back, out_specs=(VMEM, HBM),
    )
    def local_ahead(moved):
        _, late = lax.optimization_barrier((moved, wide))
        return call(local_kernel, f32(*grid_field.shape), [], grid_field, late)

    mine, other, local = from_owner(values, local_ahead)
    upstream, kept, sent = call(
        middle_kernel, (bf16(*grid_field.shape), sums, sums),
        halves_scratch,
        mine, other, local, row_back,
        jnp.asarray(depth_synthesis(pencils, True)), jnp.asarray(depth_analysis(pencils, True)), row_ahead,
    )
    received, local = to_owner(
        kept, sent, call(local_kernel, f32(*grid_field.shape), [], upstream, wide_back)
    )

    def unmix(*refs):
        unmix_kernel(kyn, *refs)

    values, back = call(
        unmix, (given, coefs), [turn_scratch],
        received, spectral_weight, plane_ahead, plane_back,
    )

    def outer(moved):
        _, late = lax.optimization_barrier((moved, back))
        return call(outer_kernel, f32(2, channels, channels, modes), [], coef, late)

    mine, other, products = from_owner(values, outer)
    return call(
        final_kernel, (bf16(*grid_field.shape), f32(2, channels, channels, modes)),
        [field_scratch, pltpu.SemaphoreType.DMA((OUTER,)), pltpu.SemaphoreType.DMA],
        mine, other, local, row_back, jnp.asarray(depth_synthesis(pencils, False)), products,
        out_specs=(HBM, HBM),
    )


def solution(mesh):
    return jax.shard_map(
        on_device,
        mesh=mesh,
        in_specs=(P(None, "slab", "yz", None), P(None, None, None, ("slab", "yz")), P()),
        out_specs=(P(None, "slab", "yz", None), P(None, None, None, ("slab", "yz"))),
        check_vma=False,
    )
```

```python
import math

import jax
import jax.numpy as jnp
import ml_dtypes
import numpy as np
from jax import lax
from jax.experimental import pallas as pl
from jax.experimental.pallas import tpu as pltpu
from jax.sharding import PartitionSpec as P

KX = 16
KY = 16
MZ = 32
NY = 256
NZ = 256
ROWS = 8
LANES = 128
PIECES = 2
OUTER = 4

GELU_SCALE = 0.7978845608028654
GELU_CUBIC = 0.044715
BF16 = ml_dtypes.bfloat16
LARGE = 54272


def freqs(number, length):
    index = np.arange(number)
    return np.where(index < number // 2, index, length - number + index)


def angles(positions, frequencies, length):
    phase = (positions[:, None].astype(np.int64) * frequencies[None, :]) % length
    return phase * (2.0 * math.pi / length)


def halves(matrix):
    matrix = np.asarray(matrix, np.float32)
    upper = matrix.astype(BF16)
    lower = (matrix - upper.astype(np.float32)).astype(BF16)
    return upper, lower


def depth_freqs(pencils):
    groups = MZ // pencils
    return np.array([[g * pencils + q for g in range(groups)] for q in range(pencils)])


def depth_analysis(pencils, doubled):
    kz = depth_freqs(pencils)
    theta = angles(kz.reshape(-1), np.arange(NZ), NZ).reshape(pencils, -1, NZ)
    weight = np.where(kz == 0, 1.0, 2.0 if doubled else 1.0)[:, :, None]
    table = np.stack([np.cos(theta) * weight, -np.sin(theta) * weight], axis=1)
    return np.concatenate(halves(table.reshape(2 * MZ, NZ)), axis=0)


def depth_synthesis(pencils, doubled):
    kz = depth_freqs(pencils)
    theta = angles(kz.reshape(-1), np.arange(NZ), NZ).reshape(pencils, -1, NZ)
    weight = np.where(kz == 0, 1.0, 2.0 if doubled else 1.0)[:, :, None]
    table = np.stack([np.cos(theta) * weight, -np.sin(theta) * weight], axis=1)
    return np.tile(table.reshape(2 * MZ, NZ), (2, 1)).astype(BF16)


def row_analysis(pencils, planes):
    rows = NY // pencils
    tables = []
    for member in range(pencils):
        theta = angles(freqs(KY, NY), member * rows + np.arange(rows), NY)
        table = np.zeros((KY, 2, planes, 2, planes, rows))
        for x in range(planes):
            table[:, 0, x, 0, x] = np.cos(theta)
            table[:, 0, x, 1, x] = np.sin(theta)
            table[:, 1, x, 0, x] = -np.sin(theta)
            table[:, 1, x, 1, x] = np.cos(theta)
        table = table.reshape(KY * 2 * planes, 2 * planes * rows)
        tables.append(np.concatenate(halves(table), axis=0))
    return np.stack(tables)


def row_synthesis(pencils, planes):
    rows = NY // pencils
    tables = []
    for member in range(pencils):
        theta = angles(freqs(KY, NY), member * rows + np.arange(rows), NY)
        table = np.zeros((KY, 2, planes, 2, planes, rows))
        for x in range(planes):
            table[:, 0, x, 0, x] = np.cos(theta)
            table[:, 1, x, 0, x] = -np.sin(theta)
            table[:, 0, x, 1, x] = np.sin(theta)
            table[:, 1, x, 1, x] = np.cos(theta)
        upper, lower = halves(table.reshape(KY * 2 * planes, 2 * planes * rows))
        tables.append(np.concatenate([upper, upper, lower], axis=0))
    return np.stack(tables)


def member_tables(pencils, planes):
    depth = depth_analysis(pencils, False)
    ahead = row_analysis(pencils, planes)
    back = row_synthesis(pencils, planes)
    return np.stack([np.concatenate([depth, ahead[q], back[q]], 0) for q in range(pencils)])


def padded(table):
    return np.pad(table, ((0, 0), (0, max(0, LANES - table.shape[1]))))


def plane_analysis(slabs, planes, kyn, scale):
    theta = angles(np.arange(slabs * planes), freqs(KX, slabs * planes), slabs * planes)
    theta = theta.reshape(slabs, planes, KX)
    table = np.zeros((slabs, kyn, 2, planes, 2, kyn, KX))
    for k in range(kyn):
        table[:, k, 0, :, 0, k] = np.cos(theta)
        table[:, k, 1, :, 0, k] = np.sin(theta)
        table[:, k, 0, :, 1, k] = -np.sin(theta)
        table[:, k, 1, :, 1, k] = np.cos(theta)
    table = scale * table.reshape(slabs * kyn * 2 * planes, 2 * kyn * KX)
    upper, lower = halves(padded(table))
    return np.concatenate([upper, upper, lower], axis=0)


def plane_synthesis(slabs, planes, kyn, scale):
    theta = angles(np.arange(slabs * planes), freqs(KX, slabs * planes), slabs * planes)
    theta = theta.reshape(slabs, planes, KX)
    table = np.zeros((slabs, kyn, 2, planes, 2, kyn, KX))
    for k in range(kyn):
        table[:, k, 0, :, 0, k] = np.cos(theta)
        table[:, k, 0, :, 1, k] = -np.sin(theta)
        table[:, k, 1, :, 0, k] = np.sin(theta)
        table[:, k, 1, :, 1, k] = np.cos(theta)
    table = scale * table.reshape(slabs * kyn * 2 * planes, 2 * kyn * KX)
    return np.stack(halves(padded(table)))


def split(value):
    upper = value.astype(jnp.bfloat16)
    return upper, (value - upper.astype(jnp.float32)).astype(jnp.bfloat16)


def dot(left, right, left_dim=1, right_dim=0):
    return lax.dot_general(
        left, right, (((left_dim,), (right_dim,)), ((), ())), preferred_element_type=jnp.float32
    )


def analyze_depth(c, block, depth_ref, upper_ref, lower_ref):
    pencils, _, width = upper_ref.shape
    width = width // 2
    groups = MZ // pencils
    depth = dot(depth_ref[...], block, 1, 1)
    depth = depth[: 2 * MZ] + depth[2 * MZ :]
    for q in range(pencils):
        base = q * 2 * groups
        lines = [
            jnp.concatenate(
                [
                    depth[base : base + groups, e * width : (e + 1) * width],
                    depth[base + groups : base + 2 * groups, e * width : (e + 1) * width],
                ],
                axis=1,
            )
            for e in range(2)
        ]
        upper, lower = split(jnp.concatenate(lines, axis=0))
        upper_ref[q, c * groups : (c + 2) * groups] = upper
        lower_ref[q, c * groups : (c + 2) * groups] = lower


def analyze_rows(row_ref, upper_ref, lower_ref, kept_ref, sent_ref):
    blocks, pencils, line, half = kept_ref.shape
    count = row_ref.shape[0] // 2
    first = lax.axis_index("yz") % 2 == 0
    for q in range(pencils):
        both = dot(row_ref[...], upper_ref[q], 1, 1)
        total = both[:count] + both[count:] + dot(row_ref[:count], lower_ref[q], 1, 1)
        low = total[:, :half].reshape(blocks, line, half)
        high = total[:, half:].reshape(blocks, line, half)
        kept_ref[:, q] = jnp.where(first, low, high)
        sent_ref[:, q] = jnp.where(first, high, low)


def fetch(hbm, ref, sem, lane=0):
    copy = pltpu.make_async_copy(hbm, ref, sem)
    copy.start(priority=lane)
    return copy


def analyze_kernel(
    grid_hbm, table_hbm, kept_ref, sent_ref, row_ref, lift_ref,
    grid_ref, depth_ref, upper_ref, lower_ref, piece_sem, table_sem,
):
    channels, planes, rows, cells = grid_hbm.shape
    step = channels // PIECES
    table = table_hbm.at[lax.axis_index("yz")]
    first = depth_ref.shape[0]
    second = first + row_ref.shape[0]
    depth_copy = fetch(table.at[pl.ds(0, first)], depth_ref, table_sem.at[0])
    pieces = [
        fetch(grid_hbm.at[pl.ds(i * step, step)], grid_ref.at[pl.ds(i * step, step)], piece_sem.at[i], i % 2)
        for i in range(PIECES)
    ]
    row_copy = fetch(table.at[pl.ds(first, row_ref.shape[0])], row_ref, table_sem.at[1])
    lift_copy = fetch(table.at[pl.ds(second, lift_ref.shape[0])], lift_ref, table_sem.at[2])
    depth_copy.wait()
    for c in range(0, channels, 2):
        if c % step == 0:
            pieces[c // step].wait()
        block = grid_ref[c : c + 2].reshape(2 * planes * rows, cells)
        analyze_depth(c, block, depth_ref, upper_ref, lower_ref)
    row_copy.wait()
    analyze_rows(row_ref, upper_ref, lower_ref, kept_ref, sent_ref)
    lift_copy.wait()


def collect(sums_ref, plane_ref, turn_ref, kyn, channels):
    slabs, pencils, line, half = sums_ref.shape
    sides = []
    for core in range(2):
        side = sums_ref[:, core]
        for member in range(core + 2, pencils, 2):
            side = side + sums_ref[:, member]
        sides.append(side.reshape(slabs * line, half))
    upper, lower = split(jnp.concatenate(sides, axis=1))
    turn_ref[...] = dot(jnp.concatenate([upper, lower, upper], axis=0), plane_ref[...], 0, 0)
    groups = 2 * half // channels
    lines = [turn_ref[pl.ds(g, channels, stride=groups)] for g in range(groups)]
    parts = []
    for part in range(2):
        pieces = []
        for k in range(kyn):
            start = (part * kyn + k) * KX
            pieces += [line[:, start : start + KX] for line in lines]
        parts.append(jnp.concatenate(pieces, axis=1) if len(pieces) > 1 else pieces[0])
    return parts


def distribute(real, imag, plane_ref, turn_ref, kyn, out_ref):
    slabs, pencils, line, half = out_ref.shape
    channels = real.shape[0]
    groups = 2 * half // channels
    for g in range(groups):
        pieces = []
        for value in (real, imag):
            for k in range(kyn):
                start = (k * groups + g) * KX
                pieces.append(value[:, start : start + KX])
        rest = turn_ref.shape[1] - 2 * kyn * KX
        if rest:
            pieces.append(jnp.zeros((channels, rest), jnp.float32))
        turn_ref[pl.ds(g, channels, stride=groups)] = jnp.concatenate(pieces, axis=1)
    upper, lower = split(turn_ref[...])
    total = (
        dot(plane_ref[0], upper, 1, 1)
        + dot(plane_ref[1], upper, 1, 1)
        + dot(plane_ref[0], lower, 1, 1)
    )
    for member in range(pencils):
        side = total[:, member % 2 * half : (member % 2 + 1) * half]
        out_ref[:, member] = side.reshape(slabs, line, half)


def mix_kernel(
    kyn, sums_ref, weight_ref, ahead_ref, back_ref, out_ref, coef_hbm, coef_ref, mixed_ref, turn_ref, sem
):
    real, imag = collect(sums_ref, ahead_ref, turn_ref, kyn, weight_ref.shape[1])
    coef_ref[0] = real
    coef_ref[1] = imag
    copy = fetch(coef_ref, coef_hbm, sem)
    for o in range(weight_ref.shape[1]):
        weight_real = weight_ref[0, o].astype(jnp.float32)
        weight_imag = weight_ref[1, o].astype(jnp.float32)
        mixed_ref[0, o : o + 1] = jnp.sum(
            weight_real * real - weight_imag * imag, axis=0, keepdims=True
        )
        mixed_ref[1, o : o + 1] = jnp.sum(
            weight_real * imag + weight_imag * real, axis=0, keepdims=True
        )
    distribute(mixed_ref[0], mixed_ref[1], back_ref, turn_ref, kyn, out_ref)
    copy.wait()


def unmix_kernel(kyn, sums_ref, weight_ref, ahead_ref, back_ref, out_ref, coef_ref, turn_ref):
    real, imag = collect(sums_ref, ahead_ref, turn_ref, kyn, weight_ref.shape[1])
    coef_ref[0] = real
    coef_ref[1] = imag
    modes_real = jnp.zeros_like(real)
    modes_imag = jnp.zeros_like(real)
    for o in range(weight_ref.shape[1]):
        weight_real = weight_ref[0, o].astype(jnp.float32)
        weight_imag = weight_ref[1, o].astype(jnp.float32)
        back_real = coef_ref[0, o : o + 1]
        back_imag = coef_ref[1, o : o + 1]
        modes_real = modes_real + (weight_real * back_real + weight_imag * back_imag)
        modes_imag = modes_imag + (weight_real * back_imag - weight_imag * back_real)
    distribute(modes_real, modes_imag, back_ref, turn_ref, kyn, out_ref)


def outer_kernel(coef_ref, back_ref, out_ref):
    real, imag = coef_ref[0], coef_ref[1]
    for o in range(back_ref.shape[1]):
        back_real = back_ref[0, o : o + 1]
        back_imag = back_ref[1, o : o + 1]
        out_ref[0, o] = back_real * real + back_imag * imag
        out_ref[1, o] = back_imag * real - back_real * imag


def lift(mine_ref, other_ref, row_ref):
    blocks, pencils, line, half = mine_ref.shape
    first = lax.axis_index("yz") % 2 == 0
    lines = []
    for q in range(pencils):
        mine = mine_ref[:, q].reshape(blocks * line, half)
        other = other_ref[:, q].reshape(blocks * line, half)
        value = jnp.concatenate(
            [jnp.where(first, mine, other), jnp.where(first, other, mine)], axis=1
        )
        upper, lower = split(value)
        stacked = jnp.concatenate([upper, lower, upper], axis=0)
        lines.append(dot(stacked, row_ref[...], 0, 0))
    return lines


def spread(lines, o):
    groups = MZ // len(lines)
    lanes = lines[0].shape[1] // 2
    block = jnp.concatenate(
        [
            line[o * groups : (o + 1) * groups, part * lanes : (part + 1) * lanes]
            for line in lines
            for part in range(2)
        ],
        axis=0,
    )
    return jnp.concatenate(split(block), axis=0).T


def local_kernel(grid_ref, wide_ref, out_ref):
    channels, planes, rows, cells = grid_ref.shape
    for x in range(planes):
        for y in range(0, rows, 2 * ROWS):
            block = grid_ref[:, x, y : y + 2 * ROWS]
            for start in (0, ROWS):
                part = block[:, start : start + ROWS].reshape(channels * ROWS, cells)
                total = dot(wide_ref[...], part).reshape(channels, ROWS, cells)
                out_ref[:, x, y + start : y + start + ROWS] = total


def middle_kernel(
    mine_ref, other_ref, local_ref, lift_ref, synth_ref, depth_ref, row_ref,
    up_ref, kept_ref, sent_ref, upper_ref, lower_ref,
):
    channels, planes, rows, cells = local_ref.shape
    lines = lift(mine_ref, other_ref, lift_ref)
    for o in range(0, channels, 2):
        blocks = []
        for e in range(o, o + 2):
            before = dot(spread(lines, e), synth_ref[...])
            before = before + local_ref[e].reshape(planes * rows, cells)
            square = before * before
            tangent = jnp.tanh(before * (GELU_SCALE + (GELU_SCALE * GELU_CUBIC) * square))
            above = 1.0 + tangent
            below = 1.0 - tangent
            quarter = 0.25 * GELU_SCALE + (0.75 * GELU_SCALE * GELU_CUBIC) * square
            upstream = (before * (above * above)) * (0.25 + (before * below) * quarter)
            blocks.append(upstream.astype(jnp.bfloat16))
            up_ref[e] = blocks[-1].reshape(planes, rows, cells)
        analyze_depth(o, jnp.concatenate(blocks, axis=0), depth_ref, upper_ref, lower_ref)
    analyze_rows(row_ref, upper_ref, lower_ref, kept_ref, sent_ref)


def final_kernel(
    mine_ref, other_ref, local_ref, lift_ref, synth_ref, product_ref, out_hbm, weight_hbm,
    result_ref, out_sems, weight_sem,
):
    channels, planes, rows, cells = local_ref.shape
    weight_copy = fetch(product_ref, weight_hbm, weight_sem, 1)
    lines = lift(mine_ref, other_ref, lift_ref)
    step = channels // OUTER
    copies = []
    for o in range(channels):
        total = dot(spread(lines, o), synth_ref[...])
        total = total + local_ref[o].reshape(planes * rows, cells)
        result_ref[o] = total.astype(jnp.bfloat16).reshape(planes, rows, cells)
        if (o + 1) % step == 0:
            part = pl.ds(o + 1 - step, step)
            copies.append(fetch(result_ref.at[part], out_hbm.at[part], out_sems.at[len(copies)]))
    for copy in [weight_copy] + copies:
        copy.wait()


VMEM = pl.BlockSpec(memory_space=pltpu.VMEM)
HBM = pl.BlockSpec(memory_space=pltpu.HBM)


def call(kernel, outs, scratch, *operands, far=(), out_specs=None, limit=20480):
    return pl.pallas_call(
        kernel,
        out_shape=outs,
        in_specs=[HBM if i in far else VMEM for i in range(len(operands))],
        out_specs=jax.tree.map(lambda _: VMEM, outs) if out_specs is None else out_specs,
        scratch_shapes=scratch,
        compiler_params=pltpu.CompilerParams(vmem_limit_bytes=limit << 10),
        cost_estimate=pl.CostEstimate(flops=1 << 30, bytes_accessed=4 << 20, transcendentals=0),
    )(*operands)


def f32(*shape):
    return jax.ShapeDtypeStruct(shape, jnp.float32)


def bf16(*shape):
    return jax.ShapeDtypeStruct(shape, jnp.bfloat16)


def on_device(grid_field, spectral_weight, local_weight):
    channels, planes, rows, cells = grid_field.shape
    slabs = lax.axis_size("slab")
    pencils = lax.axis_size("yz")
    groups = MZ // pencils
    scale = 1.0 / math.sqrt(planes * slabs * NY * NZ)
    pairs = KY * groups // slabs
    kyn = max(1, pairs // groups)
    gn = pairs // kyn
    blocks = KY // kyn
    turns = groups // gn
    half = channels // 2
    line = kyn * 2 * planes
    modes = spectral_weight.shape[3]

    table = jnp.asarray(member_tables(pencils, planes))
    plane_ahead = jnp.asarray(plane_analysis(slabs, planes, kyn, scale))
    plane_back = jnp.asarray(plane_synthesis(slabs, planes, kyn, scale))
    repeat = jnp.asarray(np.repeat(np.eye(channels), ROWS, axis=0).astype(BF16))
    mask = jnp.asarray(np.tile(np.eye(ROWS), (channels, channels)).astype(BF16))
    neighbours = [(i, i ^ 1) for i in range(pencils)]

    def widen(weight):
        rows_wide = dot(repeat, weight).astype(jnp.bfloat16)
        return dot(rows_wide, repeat, 1, 1).astype(jnp.bfloat16) * mask

    def to_owner(kept, sent, beside):
        given = lax.ppermute(sent, "yz", neighbours)
        given, beside = lax.optimization_barrier((given, beside))
        parts = kept + given
        if turns > 1:
            parts = parts.reshape(blocks, pencils, line, half, turns, gn)
            parts = jnp.transpose(parts, (0, 4, 1, 2, 3, 5))
        parts = parts.reshape(slabs * pencils, line, half * gn)
        moved = lax.all_to_all(parts, ("slab", "yz"), 0, 0, tiled=True)
        return moved.reshape(slabs, pencils, line, half * gn), beside

    def from_owner(values, work):
        values = values.reshape(slabs * pencils, line, half * gn)
        moved = lax.all_to_all(values, ("slab", "yz"), 0, 0, tiled=True)
        if turns > 1:
            moved = moved.reshape(blocks, turns, pencils, line, half, gn)
            moved = jnp.transpose(moved, (0, 2, 3, 4, 1, 5))
        moved = moved.reshape(blocks, pencils, line, half * groups)
        other = lax.ppermute(moved, "yz", neighbours)
        if work is None:
            return moved, other, None
        return lax.optimization_barrier((moved, other, work(moved)))

    halves_scratch = [pltpu.VMEM((pencils, channels * groups, 2 * planes * rows), jnp.bfloat16)] * 2
    turn_scratch = pltpu.VMEM((channels * gn, plane_ahead.shape[1]), jnp.float32)
    field_scratch = pltpu.VMEM(grid_field.shape, jnp.bfloat16)
    sums = f32(blocks, pencils, line, half * groups)
    given = f32(slabs, pencils, line, half * gn)
    coefs = f32(2, channels, modes)
    values_count = KY * 2 * planes

    kept, sent, row_ahead, row_back = call(
        analyze_kernel, (sums, sums, bf16(2 * values_count, 2 * planes * rows), bf16(3 * values_count, 2 * planes * rows)),
        [
            field_scratch, pltpu.VMEM((4 * MZ, NZ), jnp.bfloat16), *halves_scratch,
            pltpu.SemaphoreType.DMA((PIECES,)), pltpu.SemaphoreType.DMA((3,)),
        ],
        grid_field, table, far=(0, 1), limit=LARGE,
    )
    received, (wide, wide_back) = to_owner(
        kept, sent, (widen(local_weight), widen(local_weight.T))
    )

    def mix(*refs):
        mix_kernel(kyn, *refs)

    values, coef = call(
        mix, (given, coefs),
        [pltpu.VMEM((2, channels, modes), jnp.float32)] * 2 + [turn_scratch, pltpu.SemaphoreType.DMA],
        received, spectral_weight, plane_ahead, plane_back, out_specs=(VMEM, HBM),
    )
    def local_ahead(moved):
        _, late = lax.optimization_barrier((moved, wide))
        return call(local_kernel, f32(*grid_field.shape), [], grid_field, late)

    mine, other, local = from_owner(values, local_ahead)
    upstream, kept, sent = call(
        middle_kernel, (bf16(*grid_field.shape), sums, sums),
        halves_scratch,
        mine, other, local, row_back,
        jnp.asarray(depth_synthesis(pencils, True)), jnp.asarray(depth_analysis(pencils, True)), row_ahead,
    )
    received, local = to_owner(
        kept, sent, call(local_kernel, f32(*grid_field.shape), [], upstream, wide_back)
    )

    def unmix(*refs):
        unmix_kernel(kyn, *refs)

    values, back = call(
        unmix, (given, coefs), [turn_scratch],
        received, spectral_weight, plane_ahead, plane_back,
    )

    def outer(moved):
        _, late = lax.optimization_barrier((moved, back))
        return call(outer_kernel, f32(2, channels, channels, modes), [], coef, late)

    mine, other, products = from_owner(values, outer)
    return call(
        final_kernel, (bf16(*grid_field.shape), f32(2, channels, channels, modes)),
        [field_scratch, pltpu.SemaphoreType.DMA((OUTER,)), pltpu.SemaphoreType.DMA],
        mine, other, local, row_back, jnp.asarray(depth_synthesis(pencils, False)), products,
        out_specs=(HBM, HBM),
    )


def solution(mesh):
    return jax.shard_map(
        on_device,
        mesh=mesh,
        in_specs=(P(None, "slab", "yz", None), P(None, None, None, ("slab", "yz")), P()),
        out_specs=(P(None, "slab", "yz", None), P(None, None, None, ("slab", "yz"))),
        check_vma=False,
    )
```

```python
import math

import jax
import jax.numpy as jnp
import ml_dtypes
import numpy as np
from jax import lax
from jax.experimental import pallas as pl
from jax.experimental.pallas import tpu as pltpu
from jax.sharding import PartitionSpec as P

KX = 16
KY = 16
MZ = 32
NY = 256
NZ = 256
ROWS = 8
LANES = 128
PIECES = 2
OUTER = 4

GELU_SCALE = 0.7978845608028654
GELU_CUBIC = 0.044715
BF16 = ml_dtypes.bfloat16
LARGE = 54272


def freqs(number, length):
    index = np.arange(number)
    return np.where(index < number // 2, index, length - number + index)


def angles(positions, frequencies, length):
    phase = (positions[:, None].astype(np.int64) * frequencies[None, :]) % length
    return phase * (2.0 * math.pi / length)


def halves(matrix):
    matrix = np.asarray(matrix, np.float32)
    upper = matrix.astype(BF16)
    lower = (matrix - upper.astype(np.float32)).astype(BF16)
    return upper, lower


def depth_freqs(pencils):
    groups = MZ // pencils
    return np.array([[g * pencils + q for g in range(groups)] for q in range(pencils)])


def depth_analysis(pencils, doubled):
    kz = depth_freqs(pencils)
    theta = angles(kz.reshape(-1), np.arange(NZ), NZ).reshape(pencils, -1, NZ)
    weight = np.where(kz == 0, 1.0, 2.0 if doubled else 1.0)[:, :, None]
    table = np.stack([np.cos(theta) * weight, -np.sin(theta) * weight], axis=1)
    return np.concatenate(halves(table.reshape(2 * MZ, NZ)), axis=0)


def depth_synthesis(pencils, doubled):
    kz = depth_freqs(pencils)
    theta = angles(kz.reshape(-1), np.arange(NZ), NZ).reshape(pencils, -1, NZ)
    weight = np.where(kz == 0, 1.0, 2.0 if doubled else 1.0)[:, :, None]
    table = np.stack([np.cos(theta) * weight, -np.sin(theta) * weight], axis=1)
    return np.tile(table.reshape(2 * MZ, NZ), (2, 1)).astype(BF16)


def row_analysis(pencils, planes):
    rows = NY // pencils
    tables = []
    for member in range(pencils):
        theta = angles(freqs(KY, NY), member * rows + np.arange(rows), NY)
        table = np.zeros((KY, 2, planes, 2, planes, rows))
        for x in range(planes):
            table[:, 0, x, 0, x] = np.cos(theta)
            table[:, 0, x, 1, x] = np.sin(theta)
            table[:, 1, x, 0, x] = -np.sin(theta)
            table[:, 1, x, 1, x] = np.cos(theta)
        table = table.reshape(KY * 2 * planes, 2 * planes * rows)
        tables.append(np.concatenate(halves(table), axis=0))
    return np.stack(tables)


def row_synthesis(pencils, planes):
    rows = NY // pencils
    tables = []
    for member in range(pencils):
        theta = angles(freqs(KY, NY), member * rows + np.arange(rows), NY)
        table = np.zeros((KY, 2, planes, 2, planes, rows))
        for x in range(planes):
            table[:, 0, x, 0, x] = np.cos(theta)
            table[:, 1, x, 0, x] = -np.sin(theta)
            table[:, 0, x, 1, x] = np.sin(theta)
            table[:, 1, x, 1, x] = np.cos(theta)
        upper, lower = halves(table.reshape(KY * 2 * planes, 2 * planes * rows))
        tables.append(np.concatenate([upper, upper, lower], axis=0))
    return np.stack(tables)


def member_tables(pencils, planes):
    depth = depth_analysis(pencils, False)
    ahead = row_analysis(pencils, planes)
    back = row_synthesis(pencils, planes)
    return np.stack([np.concatenate([depth, ahead[q], back[q]], 0) for q in range(pencils)])


def padded(table):
    return np.pad(table, ((0, 0), (0, max(0, LANES - table.shape[1]))))


def plane_analysis(slabs, planes, kyn, scale):
    theta = angles(np.arange(slabs * planes), freqs(KX, slabs * planes), slabs * planes)
    theta = theta.reshape(slabs, planes, KX)
    table = np.zeros((slabs, kyn, 2, planes, 2, kyn, KX))
    for k in range(kyn):
        table[:, k, 0, :, 0, k] = np.cos(theta)
        table[:, k, 1, :, 0, k] = np.sin(theta)
        table[:, k, 0, :, 1, k] = -np.sin(theta)
        table[:, k, 1, :, 1, k] = np.cos(theta)
    table = scale * table.reshape(slabs * kyn * 2 * planes, 2 * kyn * KX)
    upper, lower = halves(padded(table))
    return np.concatenate([upper, upper, lower], axis=0)


def plane_synthesis(slabs, planes, kyn, scale):
    theta = angles(np.arange(slabs * planes), freqs(KX, slabs * planes), slabs * planes)
    theta = theta.reshape(slabs, planes, KX)
    table = np.zeros((slabs, kyn, 2, planes, 2, kyn, KX))
    for k in range(kyn):
        table[:, k, 0, :, 0, k] = np.cos(theta)
        table[:, k, 0, :, 1, k] = -np.sin(theta)
        table[:, k, 1, :, 0, k] = np.sin(theta)
        table[:, k, 1, :, 1, k] = np.cos(theta)
    table = scale * table.reshape(slabs * kyn * 2 * planes, 2 * kyn * KX)
    return np.stack(halves(padded(table)))


def split(value):
    upper = value.astype(jnp.bfloat16)
    return upper, (value - upper.astype(jnp.float32)).astype(jnp.bfloat16)


def dot(left, right, left_dim=1, right_dim=0):
    return lax.dot_general(
        left, right, (((left_dim,), (right_dim,)), ((), ())), preferred_element_type=jnp.float32
    )


def analyze_depth(c, block, depth_ref, upper_ref, lower_ref):
    pencils, _, width = upper_ref.shape
    width = width // 2
    groups = MZ // pencils
    depth = dot(depth_ref[...], block, 1, 1)
    depth = depth[: 2 * MZ] + depth[2 * MZ :]
    for q in range(pencils):
        base = q * 2 * groups
        lines = [
            jnp.concatenate(
                [
                    depth[base : base + groups, e * width : (e + 1) * width],
                    depth[base + groups : base + 2 * groups, e * width : (e + 1) * width],
                ],
                axis=1,
            )
            for e in range(2)
        ]
        upper_ref[q, c * groups : (c + 2) * groups] = jnp.concatenate(lines, axis=0).astype(jnp.bfloat16)


def analyze_rows(row_ref, upper_ref, lower_ref, kept_ref, sent_ref):
    blocks, pencils, line, half = kept_ref.shape
    count = row_ref.shape[0] // 2
    first = lax.axis_index("yz") % 2 == 0
    for q in range(pencils):
        both = dot(row_ref[...], upper_ref[q], 1, 1)
        total = both[:count] + both[count:]
        low = total[:, :half].reshape(blocks, line, half)
        high = total[:, half:].reshape(blocks, line, half)
        kept_ref[:, q] = jnp.where(first, low, high)
        sent_ref[:, q] = jnp.where(first, high, low)


def fetch(hbm, ref, sem, lane=0):
    copy = pltpu.make_async_copy(hbm, ref, sem)
    copy.start(priority=lane)
    return copy


def analyze_kernel(
    grid_hbm, table_hbm, kept_ref, sent_ref, row_ref, lift_ref,
    grid_ref, depth_ref, upper_ref, lower_ref, piece_sem, table_sem,
):
    channels, planes, rows, cells = grid_hbm.shape
    step = channels // PIECES
    table = table_hbm.at[lax.axis_index("yz")]
    first = depth_ref.shape[0]
    second = first + row_ref.shape[0]
    depth_copy = fetch(table.at[pl.ds(0, first)], depth_ref, table_sem.at[0])
    pieces = [
        fetch(grid_hbm.at[pl.ds(i * step, step)], grid_ref.at[pl.ds(i * step, step)], piece_sem.at[i], i % 2)
        for i in range(PIECES)
    ]
    row_copy = fetch(table.at[pl.ds(first, row_ref.shape[0])], row_ref, table_sem.at[1])
    lift_copy = fetch(table.at[pl.ds(second, lift_ref.shape[0])], lift_ref, table_sem.at[2])
    depth_copy.wait()
    for c in range(0, channels, 2):
        if c % step == 0:
            pieces[c // step].wait()
        block = grid_ref[c : c + 2].reshape(2 * planes * rows, cells)
        analyze_depth(c, block, depth_ref, upper_ref, lower_ref)
    row_copy.wait()
    analyze_rows(row_ref, upper_ref, lower_ref, kept_ref, sent_ref)
    lift_copy.wait()


def collect(sums_ref, plane_ref, turn_ref, kyn, channels):
    slabs, pencils, line, half = sums_ref.shape
    sides = []
    for core in range(2):
        side = sums_ref[:, core]
        for member in range(core + 2, pencils, 2):
            side = side + sums_ref[:, member]
        sides.append(side.reshape(slabs * line, half))
    upper, lower = split(jnp.concatenate(sides, axis=1))
    turn_ref[...] = dot(jnp.concatenate([upper, lower, upper], axis=0), plane_ref[...], 0, 0)
    groups = 2 * half // channels
    lines = [turn_ref[pl.ds(g, channels, stride=groups)] for g in range(groups)]
    parts = []
    for part in range(2):
        pieces = []
        for k in range(kyn):
            start = (part * kyn + k) * KX
            pieces += [line[:, start : start + KX] for line in lines]
        parts.append(jnp.concatenate(pieces, axis=1) if len(pieces) > 1 else pieces[0])
    return parts


def distribute(real, imag, plane_ref, turn_ref, kyn, out_ref):
    slabs, pencils, line, half = out_ref.shape
    channels = real.shape[0]
    groups = 2 * half // channels
    for g in range(groups):
        pieces = []
        for value in (real, imag):
            for k in range(kyn):
                start = (k * groups + g) * KX
                pieces.append(value[:, start : start + KX])
        rest = turn_ref.shape[1] - 2 * kyn * KX
        if rest:
            pieces.append(jnp.zeros((channels, rest), jnp.float32))
        turn_ref[pl.ds(g, channels, stride=groups)] = jnp.concatenate(pieces, axis=1)
    upper, lower = split(turn_ref[...])
    total = (
        dot(plane_ref[0], upper, 1, 1)
        + dot(plane_ref[1], upper, 1, 1)
        + dot(plane_ref[0], lower, 1, 1)
    )
    for member in range(pencils):
        side = total[:, member % 2 * half : (member % 2 + 1) * half]
        out_ref[:, member] = side.reshape(slabs, line, half)


def mix_kernel(
    kyn, sums_ref, weight_ref, ahead_ref, back_ref, out_ref, coef_hbm, coef_ref, mixed_ref, turn_ref, sem
):
    real, imag = collect(sums_ref, ahead_ref, turn_ref, kyn, weight_ref.shape[1])
    coef_ref[0] = real
    coef_ref[1] = imag
    copy = fetch(coef_ref, coef_hbm, sem)
    for o in range(weight_ref.shape[1]):
        weight_real = weight_ref[0, o].astype(jnp.float32)
        weight_imag = weight_ref[1, o].astype(jnp.float32)
        mixed_ref[0, o : o + 1] = jnp.sum(
            weight_real * real - weight_imag * imag, axis=0, keepdims=True
        )
        mixed_ref[1, o : o + 1] = jnp.sum(
            weight_real * imag + weight_imag * real, axis=0, keepdims=True
        )
    distribute(mixed_ref[0], mixed_ref[1], back_ref, turn_ref, kyn, out_ref)
    copy.wait()


def unmix_kernel(kyn, sums_ref, weight_ref, ahead_ref, back_ref, out_ref, coef_ref, turn_ref):
    real, imag = collect(sums_ref, ahead_ref, turn_ref, kyn, weight_ref.shape[1])
    coef_ref[0] = real
    coef_ref[1] = imag
    modes_real = jnp.zeros_like(real)
    modes_imag = jnp.zeros_like(real)
    for o in range(weight_ref.shape[1]):
        weight_real = weight_ref[0, o].astype(jnp.float32)
        weight_imag = weight_ref[1, o].astype(jnp.float32)
        back_real = coef_ref[0, o : o + 1]
        back_imag = coef_ref[1, o : o + 1]
        modes_real = modes_real + (weight_real * back_real + weight_imag * back_imag)
        modes_imag = modes_imag + (weight_real * back_imag - weight_imag * back_real)
    distribute(modes_real, modes_imag, back_ref, turn_ref, kyn, out_ref)


def outer_kernel(coef_ref, back_ref, out_ref):
    real, imag = coef_ref[0], coef_ref[1]
    for o in range(back_ref.shape[1]):
        back_real = back_ref[0, o : o + 1]
        back_imag = back_ref[1, o : o + 1]
        out_ref[0, o] = back_real * real + back_imag * imag
        out_ref[1, o] = back_imag * real - back_real * imag


def lift(mine_ref, other_ref, row_ref):
    blocks, pencils, line, half = mine_ref.shape
    first = lax.axis_index("yz") % 2 == 0
    lines = []
    for q in range(pencils):
        mine = mine_ref[:, q].reshape(blocks * line, half)
        other = other_ref[:, q].reshape(blocks * line, half)
        value = jnp.concatenate(
            [jnp.where(first, mine, other), jnp.where(first, other, mine)], axis=1
        )
        upper, lower = split(value)
        stacked = jnp.concatenate([upper, lower, upper], axis=0)
        lines.append(dot(stacked, row_ref[...], 0, 0))
    return lines


def spread(lines, o):
    groups = MZ // len(lines)
    lanes = lines[0].shape[1] // 2
    block = jnp.concatenate(
        [
            line[o * groups : (o + 1) * groups, part * lanes : (part + 1) * lanes]
            for line in lines
            for part in range(2)
        ],
        axis=0,
    )
    return jnp.concatenate(split(block), axis=0).T


def local_kernel(grid_ref, wide_ref, out_ref):
    channels, planes, rows, cells = grid_ref.shape
    for x in range(planes):
        for y in range(0, rows, 2 * ROWS):
            block = grid_ref[:, x, y : y + 2 * ROWS]
            for start in (0, ROWS):
                part = block[:, start : start + ROWS].reshape(channels * ROWS, cells)
                total = dot(wide_ref[...], part).reshape(channels, ROWS, cells)
                out_ref[:, x, y + start : y + start + ROWS] = total


def middle_kernel(
    mine_ref, other_ref, local_ref, lift_ref, synth_ref, depth_ref, row_ref,
    up_ref, kept_ref, sent_ref, upper_ref, lower_ref,
):
    channels, planes, rows, cells = local_ref.shape
    lines = lift(mine_ref, other_ref, lift_ref)
    for o in range(0, channels, 2):
        blocks = []
        for e in range(o, o + 2):
            before = dot(spread(lines, e), synth_ref[...])
            before = before + local_ref[e].reshape(planes * rows, cells)
            square = before * before
            tangent = jnp.tanh(before * (GELU_SCALE + (GELU_SCALE * GELU_CUBIC) * square))
            above = 1.0 + tangent
            below = 1.0 - tangent
            quarter = 0.25 * GELU_SCALE + (0.75 * GELU_SCALE * GELU_CUBIC) * square
            upstream = (before * (above * above)) * (0.25 + (before * below) * quarter)
            blocks.append(upstream.astype(jnp.bfloat16))
            up_ref[e] = blocks[-1].reshape(planes, rows, cells)
        analyze_depth(o, jnp.concatenate(blocks, axis=0), depth_ref, upper_ref, lower_ref)
    analyze_rows(row_ref, upper_ref, lower_ref, kept_ref, sent_ref)


def final_kernel(
    mine_ref, other_ref, local_ref, lift_ref, synth_ref, product_ref, out_hbm, weight_hbm,
    result_ref, out_sems, weight_sem,
):
    channels, planes, rows, cells = local_ref.shape
    weight_copy = fetch(product_ref, weight_hbm, weight_sem, 1)
    lines = lift(mine_ref, other_ref, lift_ref)
    step = channels // OUTER
    copies = []
    for o in range(channels):
        total = dot(spread(lines, o), synth_ref[...])
        total = total + local_ref[o].reshape(planes * rows, cells)
        result_ref[o] = total.astype(jnp.bfloat16).reshape(planes, rows, cells)
        if (o + 1) % step == 0:
            part = pl.ds(o + 1 - step, step)
            copies.append(fetch(result_ref.at[part], out_hbm.at[part], out_sems.at[len(copies)]))
    for copy in [weight_copy] + copies:
        copy.wait()


VMEM = pl.BlockSpec(memory_space=pltpu.VMEM)
HBM = pl.BlockSpec(memory_space=pltpu.HBM)


def call(kernel, outs, scratch, *operands, far=(), out_specs=None, limit=20480):
    return pl.pallas_call(
        kernel,
        out_shape=outs,
        in_specs=[HBM if i in far else VMEM for i in range(len(operands))],
        out_specs=jax.tree.map(lambda _: VMEM, outs) if out_specs is None else out_specs,
        scratch_shapes=scratch,
        compiler_params=pltpu.CompilerParams(vmem_limit_bytes=limit << 10),
        cost_estimate=pl.CostEstimate(flops=1 << 30, bytes_accessed=4 << 20, transcendentals=0),
    )(*operands)


def f32(*shape):
    return jax.ShapeDtypeStruct(shape, jnp.float32)


def bf16(*shape):
    return jax.ShapeDtypeStruct(shape, jnp.bfloat16)


def on_device(grid_field, spectral_weight, local_weight):
    channels, planes, rows, cells = grid_field.shape
    slabs = lax.axis_size("slab")
    pencils = lax.axis_size("yz")
    groups = MZ // pencils
    scale = 1.0 / math.sqrt(planes * slabs * NY * NZ)
    pairs = KY * groups // slabs
    kyn = max(1, pairs // groups)
    gn = pairs // kyn
    blocks = KY // kyn
    turns = groups // gn
    half = channels // 2
    line = kyn * 2 * planes
    modes = spectral_weight.shape[3]

    table = jnp.asarray(member_tables(pencils, planes))
    plane_ahead = jnp.asarray(plane_analysis(slabs, planes, kyn, scale))
    plane_back = jnp.asarray(plane_synthesis(slabs, planes, kyn, scale))
    repeat = jnp.asarray(np.repeat(np.eye(channels), ROWS, axis=0).astype(BF16))
    mask = jnp.asarray(np.tile(np.eye(ROWS), (channels, channels)).astype(BF16))
    neighbours = [(i, i ^ 1) for i in range(pencils)]

    def widen(weight):
        rows_wide = dot(repeat, weight).astype(jnp.bfloat16)
        return dot(rows_wide, repeat, 1, 1).astype(jnp.bfloat16) * mask

    def to_owner(kept, sent, beside):
        given = lax.ppermute(sent, "yz", neighbours)
        given, beside = lax.optimization_barrier((given, beside))
        parts = kept + given
        if turns > 1:
            parts = parts.reshape(blocks, pencils, line, half, turns, gn)
            parts = jnp.transpose(parts, (0, 4, 1, 2, 3, 5))
        parts = parts.reshape(slabs * pencils, line, half * gn)
        moved = lax.all_to_all(parts, ("slab", "yz"), 0, 0, tiled=True)
        return moved.reshape(slabs, pencils, line, half * gn), beside

    def from_owner(values, work):
        values = values.reshape(slabs * pencils, line, half * gn)
        moved = lax.all_to_all(values, ("slab", "yz"), 0, 0, tiled=True)
        if turns > 1:
            moved = moved.reshape(blocks, turns, pencils, line, half, gn)
            moved = jnp.transpose(moved, (0, 2, 3, 4, 1, 5))
        moved = moved.reshape(blocks, pencils, line, half * groups)
        other = lax.ppermute(moved, "yz", neighbours)
        if work is None:
            return moved, other, None
        return lax.optimization_barrier((moved, other, work(moved)))

    halves_scratch = [pltpu.VMEM((pencils, channels * groups, 2 * planes * rows), jnp.bfloat16)] * 2
    turn_scratch = pltpu.VMEM((channels * gn, plane_ahead.shape[1]), jnp.float32)
    field_scratch = pltpu.VMEM(grid_field.shape, jnp.bfloat16)
    sums = f32(blocks, pencils, line, half * groups)
    given = f32(slabs, pencils, line, half * gn)
    coefs = f32(2, channels, modes)
    values_count = KY * 2 * planes

    kept, sent, row_ahead, row_back = call(
        analyze_kernel, (sums, sums, bf16(2 * values_count, 2 * planes * rows), bf16(3 * values_count, 2 * planes * rows)),
        [
            field_scratch, pltpu.VMEM((4 * MZ, NZ), jnp.bfloat16), *halves_scratch,
            pltpu.SemaphoreType.DMA((PIECES,)), pltpu.SemaphoreType.DMA((3,)),
        ],
        grid_field, table, far=(0, 1), limit=LARGE,
    )
    received, (wide, wide_back) = to_owner(
        kept, sent, (widen(local_weight), widen(local_weight.T))
    )

    def mix(*refs):
        mix_kernel(kyn, *refs)

    values, coef = call(
        mix, (given, coefs),
        [pltpu.VMEM((2, channels, modes), jnp.float32)] * 2 + [turn_scratch, pltpu.SemaphoreType.DMA],
        received, spectral_weight, plane_ahead, plane_back, out_specs=(VMEM, HBM),
    )
    def local_ahead(moved):
        _, late = lax.optimization_barrier((moved, wide))
        return call(local_kernel, f32(*grid_field.shape), [], grid_field, late)

    mine, other, local = from_owner(values, local_ahead)
    upstream, kept, sent = call(
        middle_kernel, (bf16(*grid_field.shape), sums, sums),
        halves_scratch,
        mine, other, local, row_back,
        jnp.asarray(depth_synthesis(pencils, True)), jnp.asarray(depth_analysis(pencils, True)), row_ahead,
    )
    received, local = to_owner(
        kept, sent, call(local_kernel, f32(*grid_field.shape), [], upstream, wide_back)
    )

    def unmix(*refs):
        unmix_kernel(kyn, *refs)

    values, back = call(
        unmix, (given, coefs), [turn_scratch],
        received, spectral_weight, plane_ahead, plane_back,
    )

    def outer(moved):
        _, late = lax.optimization_barrier((moved, back))
        return call(outer_kernel, f32(2, channels, channels, modes), [], coef, late)

    mine, other, products = from_owner(values, outer)
    return call(
        final_kernel, (bf16(*grid_field.shape), f32(2, channels, channels, modes)),
        [field_scratch, pltpu.SemaphoreType.DMA((OUTER,)), pltpu.SemaphoreType.DMA],
        mine, other, local, row_back, jnp.asarray(depth_synthesis(pencils, False)), products,
        out_specs=(HBM, HBM),
    )


def solution(mesh):
    return jax.shard_map(
        on_device,
        mesh=mesh,
        in_specs=(P(None, "slab", "yz", None), P(None, None, None, ("slab", "yz")), P()),
        out_specs=(P(None, "slab", "yz", None), P(None, None, None, ("slab", "yz"))),
        check_vma=False,
    )
```
